32 devices in a mesh: clip: 4 (over y, x), py: 4 (over z), px: 2 (over core).
Axes of the slice: x: 2, y: 2, z: 4, core: 2. Of those that a mesh axis runs over, the one named last changes fastest.
Arguments:
- fsq_codes: int32 [6, 8, 64, 64], P(None, 'clip', 'py', 'px'), parts along dimension 1, may hold values from 0 to 7, as said below
- in_weight: bfloat16 [3, 3, 6, 512], replicated, may hold values from -0.875 to 0.875
- res_weight: bfloat16 [512, 3, 3, 512], P(('py', 'px')), may hold values from -0.09375 to 0.09375
- up_weight: bfloat16 [512, 4, 4, 512], P(('py', 'px')), may hold values from -0.125 to 0.125
- first_gain: float32 [512], replicated, may hold values from 0.1 to 1.9
- second_gain: float32 [512], replicated, may hold values from 0.1 to 1.9
Outputs:
- upsampled: bfloat16 [8, 128, 128, 512], P('clip', 'py', 'px'), parts along dimension 0
The draws below stay inside these ranges and needn't reach their ends.
There are 4 independent parts, one for each index of `clip`. The reference program is written for one: setup_inputs(seed, part) draws one part's arguments, and reference() takes and returns one part's arrays. A program takes and returns all parts, laid end to end along the dimension named above; an argument that names none is the same for every part. Nothing has to cross between parts.
Inputs may be any that keep to these rules, and one draw needn't show every extreme that they name: `fsq_codes`: entry d of the first dimension is a level index of FSQ dimension d, below 8 for d = 0, 1, 2 and below 5 for d = 3, 4, 5.
All inputs are finite; a program needn't handle non-finite values.
Results may differ from the reference program's by a relative error of at most 0.0073.
Values may be sent and summed in bfloat16 or wider, within the bound.
No kernel may reach another device: no remote copies, remote signals or barrier semaphores. Data moves between devices by JAX's collectives and lax.ppermute only.
A program may use at most 128 MiB of HBM per device.

```python
import jax
import jax.numpy as jnp
from jax import lax

C = 512
LEVELS = 6
GROUPS = 32
FRAMES = 2
CH = 16
CW = 32
HEIGHT = 64
WIDTH = 64


def draw_fsq_codes(key, part):
    key = jax.random.fold_in(key, 7)
    base_key, tile_key, pick_key, code_key = jax.random.split(key, 4)
    levels = jnp.array([8, 8, 8, 5, 5, 5], jnp.int32).reshape(LEVELS, 1, 1, 1)
    span_levels = levels // 2 + 1
    room = levels - span_levels
    base = jax.random.randint(base_key, (LEVELS, 1, 1, 1), 0, room + 1, jnp.int32)
    tile_rows = HEIGHT // CH
    tile_cols = WIDTH // CW
    tile_shift = jax.random.randint(tile_key, (LEVELS, FRAMES, tile_rows, tile_cols), -1, 2, jnp.int32)
    tile_low = jnp.clip(base + tile_shift, 0, room)
    tile_count = FRAMES * tile_rows * tile_cols
    tile_id = lax.broadcasted_iota(jnp.int32, (1, FRAMES, tile_rows, tile_cols), 1) * (tile_rows * tile_cols)
    tile_id = tile_id + lax.broadcasted_iota(jnp.int32, (1, FRAMES, tile_rows, tile_cols), 2) * tile_cols
    tile_id = tile_id + lax.broadcasted_iota(jnp.int32, (1, FRAMES, tile_rows, tile_cols), 3)
    top_tile = jax.random.randint(pick_key, (), 0, tile_count, jnp.int32)
    bottom_tile = (top_tile + tile_count // 2) % tile_count
    tile_low = jnp.where(tile_id == top_tile, room, tile_low)
    tile_low = jnp.where(tile_id == bottom_tile, 0, tile_low)
    lowest = jnp.repeat(jnp.repeat(tile_low, CH, axis=2), CW, axis=3)
    highest = lowest + span_levels
    return jax.random.randint(code_key, (LEVELS, FRAMES, HEIGHT, WIDTH), lowest, highest, jnp.int32)


def block_scale(key, shape, pieces, low, top_value):
    level = 1.0
    for position, parts in pieces:
        steps = jax.random.uniform(jax.random.fold_in(jax.random.fold_in(key, 6), position), (parts,), jnp.float32, low / len(pieces), top_value / len(pieces))
        level = level * jnp.repeat(jnp.exp(steps), shape[position] // parts).reshape((-1,) + (1,) * (len(shape) - 1 - position))
    return level


def scatter_about(own_key, dims, deviation, reach, shards=(), held_as=jnp.bfloat16):
    entries = jax.random.normal(own_key, dims, jnp.float32) * deviation
    if len(shards) > 0:
        entries = block_scale(own_key, dims, shards, -0.22, 0.18) * entries
    return jnp.clip(entries, min=-reach, max=reach).astype(held_as)


def setup_inputs(seed: int = 0, part: int = 0) -> dict:
    streams_of = jax.random.split(jax.random.key(seed), 7)
    own_keys = jax.random.split(jax.random.fold_in(streams_of[6], part), 7)
    fsq_codes = draw_fsq_codes(jax.random.fold_in(jax.random.fold_in(streams_of[6], part), 71), part)
    in_weight = scatter_about(streams_of[1], (3, 3, LEVELS, C), (9 * LEVELS) ** -0.5, 0.875)
    res_weight = scatter_about(streams_of[2], (C, 3, 3, C), (9 * C) ** -0.5, 0.09375, ((0, 8),))
    up_weight = scatter_about(streams_of[3], (C, 4, 4, C), (4 * C) ** -0.5, 0.125, ((0, 8),))
    first_gain = jnp.clip(1.0 + 0.18 * jax.random.normal(streams_of[4], (C,), jnp.float32), 0.1, 1.9)
    second_gain = jnp.clip(1.0 + 0.18 * jax.random.normal(streams_of[5], (C,), jnp.float32), 0.1, 1.9)
    return dict(fsq_codes=fsq_codes, in_weight=in_weight, res_weight=res_weight, up_weight=up_weight, first_gain=first_gain, second_gain=second_gain)


fsq_levels = (8, 8, 8, 5, 5, 5)
epsilon = 1e-06
up_taps = (((1, 1), (3, 0)), ((0, 2), (2, 1)))

def code_values(fsq_codes):
    levels = jnp.array(fsq_levels, jnp.int32).reshape(-1, 1, 1, 1)
    half_range = levels // 2
    values = (fsq_codes - half_range).astype(jnp.float32) / half_range.astype(jnp.float32)
    return jnp.transpose(values, (1, 2, 3, 0)).astype(jnp.bfloat16)

def pad_image(source):
    return jnp.pad(source, ((0, 0), (1, 1), (1, 1), (0, 0)))

def first_conv(padded, in_weight):
    out_rows = padded.shape[1] - 2
    out_cols = padded.shape[2] - 2
    windows = [padded[:, row_tap:row_tap + out_rows, col_tap:col_tap + out_cols, :] for row_tap in range(3) for col_tap in range(3)]
    stacked = jnp.concatenate(windows, axis=3)
    flat_weight = in_weight.reshape(-1, in_weight.shape[3])
    product = jnp.dot(stacked.reshape(-1, flat_weight.shape[0]), flat_weight, preferred_element_type=jnp.float32)
    return product.reshape(padded.shape[0], out_rows, out_cols, -1).astype(jnp.bfloat16)

def group_norm(source, gain_vec):
    channels = source.shape[3]
    grouped = source.astype(jnp.float32).reshape(-1, GROUPS, channels // GROUPS)
    average = lax.optimization_barrier(jnp.mean(grouped, axis=(0, 2)))
    centred = grouped - average[None, :, None]
    spread = lax.optimization_barrier(jnp.mean(centred * centred, axis=(0, 2)))
    inv_std = lax.rsqrt(spread + epsilon)
    average_c = jnp.repeat(average, channels // GROUPS)
    scale_c = jnp.repeat(inv_std, channels // GROUPS)
    normed = (source.astype(jnp.float32) - average_c) * (scale_c * gain_vec)
    return jax.nn.silu(normed)

def tap_product(window, weight_tap):
    flat = window.reshape(-1, window.shape[3])
    return jnp.dot(flat, weight_tap, preferred_element_type=jnp.float32).reshape(window.shape[:3] + (weight_tap.shape[1],))

def reference(fsq_codes, in_weight, res_weight, up_weight, first_gain, second_gain):
    values = code_values(fsq_codes)
    features = first_conv(pad_image(values), in_weight)
    frames, out_rows, out_cols, channels = features.shape
    active = group_norm(features, first_gain).astype(jnp.bfloat16)
    padded = pad_image(active)
    branch = jnp.zeros((frames, out_rows, out_cols, channels), jnp.float32)
    for row_tap in range(3):
        for col_tap in range(3):
            window = padded[:, row_tap:row_tap + out_rows, col_tap:col_tap + out_cols, :]
            branch = branch + tap_product(window, res_weight[:, row_tap, col_tap, :])
    hidden = (features.astype(jnp.float32) + branch).astype(jnp.bfloat16)
    second = group_norm(hidden, second_gain).astype(jnp.bfloat16)
    padded = pad_image(second)
    phases = []
    for row_phase in range(2):
        for col_phase in range(2):
            phase_sum = jnp.zeros((frames, out_rows, out_cols, channels), jnp.float32)
            for row_kernel, row_offset in up_taps[row_phase]:
                for col_kernel, col_offset in up_taps[col_phase]:
                    window = padded[:, row_offset:row_offset + out_rows, col_offset:col_offset + out_cols, :]
                    phase_sum = phase_sum + tap_product(window, up_weight[:, row_kernel, col_kernel, :])
            phases.append(phase_sum.astype(jnp.bfloat16))
    stacked = jnp.stack(phases).reshape(2, 2, frames, out_rows, out_cols, channels)
    return jnp.transpose(stacked, (2, 3, 0, 4, 1, 5)).reshape(frames, 2 * out_rows, 2 * out_cols, channels)
```

```python
import jax
import jax.numpy as jnp
import numpy as np
from jax import lax
from jax.experimental import pallas as pl
from jax.experimental.pallas import tpu as pltpu
from jax.sharding import PartitionSpec as P

GROUPS = 32

fsq_levels = (8, 8, 8, 5, 5, 5)
epsilon = 1e-06
VMEM_LIMIT = 56 << 20
up_taps = (((1, 1), (3, 0)), ((0, 2), (2, 1)))

COL = 40


def axis_gather(cells, axis, dim):
    count = lax.axis_size(axis)
    me = lax.axis_index(axis)
    step = 1
    while step < count:
        other = lax.ppermute(cells, axis, [(i, i ^ step) for i in range(count)])
        upper = (me & step) != 0
        low = jnp.where(upper, other, cells)
        high = jnp.where(upper, cells, other)
        cells = jnp.concatenate([low, high], axis=dim)
        step *= 2
    return cells


def code_values(fsq_codes):
    levels = jnp.array(fsq_levels, jnp.int32).reshape(-1, 1, 1, 1)
    half_range = levels // 2
    values = (fsq_codes - half_range).astype(jnp.float32) / half_range.astype(jnp.float32)
    return values.astype(jnp.bfloat16)


def lanes_up(count):
    return (count + 127) // 128 * 128


def flat_inputs(values, rows, cols):
    dims, frames, height, width = values.shape
    py = lax.axis_index("py")
    px = lax.axis_index("px")
    clip = jnp.pad(values, ((0, 0), (0, 0), (1, 1), (1, 1)))
    inside = np.zeros((1, frames, height + 2, width + 2), np.float32)
    inside[:, :, :height, :width] = 1.0
    clip = jnp.concatenate([clip, jnp.asarray(inside, jnp.bfloat16), jnp.zeros_like(clip[:1])], axis=0)
    clip = clip.reshape(8, -1)
    clip = jnp.pad(clip, ((0, 0), (0, lanes_up(clip.shape[1]) - clip.shape[1])))

    wide = jnp.pad(values, ((0, 0), (0, 0), (3, 3), (3, 3)))
    patch = lax.dynamic_slice(
        wide, (0, 0, py * rows, px * cols), (dims, frames, rows + 6, cols + 6)
    )
    y = py * rows - 2 + jnp.arange(rows + 6)[:, None]
    x = px * cols - 2 + jnp.arange(cols + 6)[None, :]
    valid = (y >= 0) & (y < height) & (x >= 0) & (x < width)
    valid = jnp.broadcast_to(valid, (1, frames, rows + 6, cols + 6)).astype(jnp.bfloat16)
    patch = jnp.concatenate([patch, valid, jnp.zeros_like(valid)], axis=0)
    patch = jnp.pad(patch, ((0, 0), (0, 0), (0, 0), (0, COL - cols - 6)))
    patch = jnp.transpose(patch, (0, 2, 1, 3)).reshape(8, -1)
    return clip.astype(jnp.float32), patch.astype(jnp.float32)


def group_mean(row):
    lane = lax.broadcasted_iota(jnp.int32, row.shape, 1)
    width = row.shape[1]
    for step in (1, 2, 4, 8):
        row = row + jnp.where(
            (lane & step) != 0, pltpu.roll(row, step, 1), pltpu.roll(row, width - step, 1)
        )
    return row * (1.0 / 16.0)


def silu(t):
    return t * (0.5 * jnp.tanh(0.5 * t) + 0.5)


def tap_rows(flat, stride, keep=None):
    width = flat.shape[1]
    parts = []
    for tap in range(9):
        shift = (tap // 3) * stride + tap % 3
        part = flat if shift == 0 else pltpu.roll(flat, width - shift, 1)
        parts.append(part if keep is None else part * keep)
    parts.append(jnp.zeros_like(flat))
    return [
        jnp.concatenate(parts[2 * i : 2 * i + 2], axis=0).astype(jnp.bfloat16) for i in range(5)
    ]


def prep_kernel(clip_stride, rows, clip_ref, patch_ref, w_ref, gain_ref, act_ref, feat_ref, mark_ref, taps, wide):
    channels = feat_ref.shape[1]
    row_len = 2 * COL
    for i, part in enumerate(tap_rows(clip_ref[...], clip_stride, clip_ref[6:7, :])):
        taps[16 * i : 16 * i + 16, :] = part
    moments = lax.dot_general(
        taps[...], taps[...], (((1,), (1,)), ((), ())), preferred_element_type=jnp.float32
    )
    total = moments[6:7, 6:7]
    mean_row = moments[6:7, :] / total
    mean_col = moments[:, 6:7] / total
    centred = moments / total - mean_col * mean_row
    weight = w_ref[:, :channels]
    weight32 = weight.astype(jnp.float32)
    spread_c = jnp.sum(
        weight32
        * jnp.dot(
            centred, weight32, precision=lax.Precision.HIGHEST, preferred_element_type=jnp.float32
        ),
        axis=0,
        keepdims=True,
    )
    mean_c = jnp.sum(weight32 * mean_col, axis=0, keepdims=True)
    mean_c = jnp.broadcast_to(mean_c, (8, channels))
    spread_c = jnp.broadcast_to(spread_c, (8, channels))
    average = group_mean(mean_c)
    apart = mean_c - average
    spread = jnp.maximum(group_mean(spread_c + apart * apart), 0.0)
    scale = (lax.rsqrt(spread + epsilon) * gain_ref[...])[0:1, :]
    average = average[0:1, :]

    patch = patch_ref[...]
    span = patch.shape[1]
    window = jnp.concatenate(tap_rows(patch, row_len), axis=0)
    block = 256
    for start in range(0, span, block):
        size = min(block, span - start)
        product = lax.dot_general(
            window[:, start : start + size],
            w_ref[...],
            (((0,), (0,)), ((), ())),
            preferred_element_type=jnp.float32,
        )
        keep = product[:, channels : channels + 128]
        feat = product[:, :channels].astype(jnp.bfloat16).astype(jnp.float32)
        active = silu((feat - average) * scale)
        for lane in range(0, channels, 128):
            wide[start : start + size, lane : lane + 128] = active[:, lane : lane + 128] * keep
    mark_ref[...] = jnp.broadcast_to(scale[:, 0:128], mark_ref.shape)
    count = act_ref.shape[0]
    for shift in range(3):
        act_ref[:, shift * channels : (shift + 1) * channels] = wide[
            shift : shift + count, :
        ].astype(jnp.bfloat16)
    moved = pltpu.roll(patch, span - (row_len + 1), 1)
    window = jnp.concatenate(tap_rows(moved, row_len), axis=0)
    inner = feat_ref.shape[0]
    for start in range(0, inner, block):
        size = min(block, inner - start)
        product = lax.dot_general(
            window[:, start : start + block],
            weight,
            (((0,), (0,)), ((), ())),
            preferred_element_type=jnp.float32,
        )
        feat_ref[start : start + size, :] = product[:size].astype(jnp.bfloat16)


def prep(values, in_weight, gain, rows, cols, waits=()):
    channels = in_weight.shape[3]
    dims, frames, height, width = values.shape
    clip, patch = flat_inputs(values, rows, cols)
    span = patch.shape[1]
    pad = lanes_up(span + 2) - span
    patch = jnp.pad(patch, ((0, 0), (0, pad)))
    clip, patch = after((clip, patch), *waits)
    weight = jnp.pad(in_weight.reshape(9, dims, channels), ((0, 1), (0, 8 - dims), (0, 128)))
    marks = np.zeros((10, 8, channels + 128), np.float32)
    marks[0, 6, channels:] = 1.0
    weight = (weight + jnp.asarray(marks, jnp.bfloat16)).reshape(80, channels + 128)
    row_len = frames * COL
    return pl.pallas_call(
        lambda *refs: prep_kernel(width + 2, rows, *refs),
        out_shape=(
            jax.ShapeDtypeStruct(((rows + 4) * row_len, 3 * channels), jnp.bfloat16),
            jax.ShapeDtypeStruct(((rows + 2) * row_len, channels), jnp.bfloat16),
            jax.ShapeDtypeStruct((8, 128), jnp.float32),
        ),
        scratch_shapes=[
            pltpu.VMEM((80, clip.shape[1]), jnp.bfloat16),
            pltpu.VMEM((patch.shape[1], channels), jnp.float32),
        ],
        compiler_params=pltpu.CompilerParams(vmem_limit_bytes=(24 << 20) + 512 * clip.shape[1]),
        name="prep",
    )(clip, patch, weight, gain.reshape(1, channels))


def conv1_kernel(copy_plan, rows, cols, *refs):
    act_hbm, feat_hbm, *sources, hid_ref, stat_ref, weight, act, feat, total, sems, in_sem = refs
    row_len = 2 * COL
    inputs = [
        pltpu.make_async_copy(act_hbm, act, in_sem.at[0]),
        pltpu.make_async_copy(feat_hbm, feat, in_sem.at[1]),
    ]
    copies = [copy_plan(sources, weight, sems, 3 * i, 3) for i in range(3)]
    for copy in inputs + copies[0]:
        copy.start()
    for copy in inputs:
        copy.wait()
    channels = feat.shape[1]
    count = hid_ref.shape[0]
    group = count
    for row_tap in range(3):
        for copy in copies[row_tap]:
            copy.wait()
        if row_tap < 2:
            for copy in copies[row_tap + 1]:
                copy.start()
        taps = weight[3 * row_tap : 3 * row_tap + 3].reshape(3 * channels, channels)
        for start in range(0, count, group):
            size = min(group, count - start)
            first = start + row_tap * row_len
            product = jnp.dot(
                act[first : first + size, :], taps, preferred_element_type=jnp.float32
            )
            if row_tap == 0:
                total[start : start + size, :] = product + feat[start : start + size, :]
            elif row_tap == 1:
                total[start : start + size, :] += product
            else:
                hid_ref[start : start + size, :] = (total[start : start + size, :] + product).astype(
                    jnp.bfloat16
                )

    place = lax.broadcasted_iota(jnp.int32, (row_len, 128), 0)
    place = jnp.where(place >= COL, place - COL, place)
    keep = ((place >= 1) & (place <= cols)).astype(jnp.float32)
    keep = jnp.concatenate([keep] * (channels // 128), axis=1)
    lines = range(row_len, (rows + 1) * row_len, row_len)
    cells = 2.0 * rows * cols
    mean = jnp.zeros((row_len, channels), jnp.float32)
    for line in lines:
        mean = mean + hid_ref[line : line + row_len, :].astype(jnp.float32)
    mean = jnp.sum(mean * keep, axis=0, keepdims=True) / cells
    square = jnp.zeros((row_len, channels), jnp.float32)
    for line in lines:
        apart = hid_ref[line : line + row_len, :].astype(jnp.float32) - mean
        square = square + apart * apart
    stat_ref[0:1, :] = mean
    stat_ref[1:2, :] = jnp.sum(square * keep, axis=0, keepdims=True)
    stat_ref[2:8, :] = jnp.zeros((6, channels), jnp.float32)


def conv2_kernel(copy_plan, rows, cols, edge_ref, hid_ref, stat_ref, gain_ref, *refs):
    *sources, out_ref, weight, wide, shifted, woven, result, sems, out_sem = refs
    row_len = 2 * COL
    channels = hid_ref.shape[1]
    copies = copy_plan(sources, weight, sems, 0, 16)
    for copy in copies:
        copy.start()

    parts = stat_ref.shape[0]
    cells = 2.0 * rows * cols
    means = stat_ref[:, 0, :]
    average_c = jnp.sum(means, axis=0, keepdims=True) / parts
    apart = means - average_c
    square_c = jnp.sum(stat_ref[:, 1, :] + cells * apart * apart, axis=0, keepdims=True)
    average_c = jnp.broadcast_to(average_c, (8, channels))
    spread_c = jnp.broadcast_to(square_c, (8, channels)) / (cells * parts)
    average = group_mean(average_c)
    apart = average_c - average
    spread = group_mean(spread_c + apart * apart)
    scale = (lax.rsqrt(spread + epsilon) * gain_ref[...])[0:1, :]
    average = average[0:1, :]

    place = lax.broadcasted_iota(jnp.int32, (row_len, channels), 0)
    place = jnp.where(place >= COL, place - COL, place)
    top, bottom, left, right = (edge_ref[i].astype(jnp.float32) for i in range(4))
    keep = jnp.where(place == 0, left, jnp.where(place == cols + 1, right, 1.0))

    def normalise(line, _):
        first = pl.multiple_of(line * row_len, row_len)
        t = (hid_ref[pl.ds(first, row_len), :].astype(jnp.float32) - average) * scale
        row_keep = jnp.where(line == 0, top, jnp.where(line == rows + 1, bottom, 1.0))
        wide[...] = silu(t) * (keep * row_keep)
        for shift in range(3):
            for frame in range(2):
                to = pl.multiple_of(line * (2 * cols) + frame * cols, cols)
                shifted[pl.ds(to, cols), shift * channels : (shift + 1) * channels] = wide[
                    frame * COL + shift : frame * COL + shift + cols, :
                ].astype(jnp.bfloat16)
        return 0

    lax.fori_loop(0, rows + 2, normalise, 0)
    for copy in copies:
        copy.wait()

    step = 8
    size = step * 2 * cols

    for part in range(rows // step):
        line = part * step
        for row_phase in range(2):
            for col_phase in range(2):
                acc = None
                for row_kernel, row_offset in up_taps[row_phase]:
                    first = (line + row_offset) * (2 * cols)
                    tap = 4 * row_kernel + 2 * col_phase
                    product = jnp.dot(
                        shifted[
                            pl.ds(first, size), col_phase * channels : (col_phase + 2) * channels
                        ],
                        weight[tap : tap + 2].reshape(2 * channels, channels),
                        preferred_element_type=jnp.float32,
                    )
                    acc = product if acc is None else acc + product
                for lane in range(channels // 128):
                    woven[row_phase, lane, pl.ds(col_phase, size, stride=2), :] = acc[
                        :, 128 * lane : 128 * lane + 128
                    ]
            for y in range(step):
                for frame in range(2):
                    at = (2 * y + frame) * 2 * cols
                    for lane in range(channels // 128):
                        result[
                            frame,
                            2 * (line + y) + row_phase,
                            :,
                            128 * lane : 128 * lane + 128,
                        ] = woven[row_phase, lane, at : at + 2 * cols, :].astype(jnp.bfloat16)
        for frame in range(2):
            lines = pl.ds(2 * line, 2 * step)
            pltpu.make_async_copy(
                result.at[frame, lines], out_ref.at[frame, lines], out_sem.at[part, frame]
            ).start()
    for part in range(rows // step):
        for frame in range(2):
            lines = pl.ds(2 * step * part, 2 * step)
            pltpu.make_async_copy(
                result.at[frame, lines], out_ref.at[frame, lines], out_sem.at[part, frame]
            ).wait()


def xor_pairs(axis, bits):
    return [(i, i ^ bits) for i in range(lax.axis_size(axis))]


def tap_major(weight):
    return jnp.transpose(weight, (1, 2, 0, 3)).reshape(-1, weight.shape[0], weight.shape[3])


def paired_taps(weight):
    rows, _, _, width = weight.shape
    halves = weight.reshape(rows, 4, 2, 2, width)[:, :, ::-1, ::-1, :]
    return jnp.transpose(halves, (1, 3, 2, 0, 4)).reshape(16, rows, width)


def column_part(weight):
    width = weight.shape[2] // lax.axis_size("clip")
    return lax.dynamic_slice_in_dim(weight, lax.axis_index("clip") * width, width, axis=2)


def swap(piece):
    return lax.ppermute(piece, "px", xor_pairs("px", 1))


def whole_gather(weight):
    def plan(sources, weight, sems, first, taps):
        taps = pl.ds(first, taps)
        return [pltpu.make_async_copy(sources[0].at[taps], weight.at[taps], sems.at[first, 0])]

    return [lax.all_gather(weight, ("py", "px"), axis=1, tiled=True)], plan


def after(held, *waits):
    return lax.optimization_barrier((held, waits))[0]


def to_z(part, bits):
    return lax.ppermute(part, "py", xor_pairs("py", bits))


def to_clips(piece):
    return [piece] + [lax.ppermute(piece, "clip", xor_pairs("clip", d)) for d in (1, 2, 3)]


def both_cores(pieces):
    return [one for piece in pieces for one in (piece, swap(piece))]


def placed_plan(placed):
    sources = []
    for entry in placed:
        if not any(entry[0] is source for source in sources):
            sources.append(entry[0])
    slots = [next(i for i, source in enumerate(sources) if source is entry[0]) for entry in placed]

    def plan(refs, weight, sems, first, taps):
        core, z, clip = lax.axis_index("px"), lax.axis_index("py"), lax.axis_index("clip")
        taps = pl.ds(first, taps)
        copies = []
        for i, (slot, (_, lead, z_bits, clip_bits, core_bit)) in enumerate(zip(slots, placed)):
            ref = refs[slot]
            rows, width = ref.shape[-2:]
            row = pl.ds(pl.multiple_of((2 * (z ^ z_bits) + (core ^ core_bit)) * rows, rows), rows)
            if clip_bits is None:
                to = weight.at[taps, row, :]
            elif clip_bits >= 0:
                to = weight.at[
                    taps, row, pl.ds(pl.multiple_of((clip ^ clip_bits) * width, width), width)
                ]
            else:
                to = weight.at[taps, row, pl.ds(-(clip_bits + 1) * width, width)]
            copies.append(
                pltpu.make_async_copy(ref.at[(*lead, taps)], to, sems.at[first, i])
            )
        return copies

    return sources, plan


def code_gather(values):
    if lax.axis_size("py") != 4 or lax.axis_size("px") != 2:
        return axis_gather(axis_gather(values, "px", 3), "py", 2), values
    z, core = lax.axis_index("py"), lax.axis_index("px")
    dense = values.reshape(values.shape[0] * values.shape[1], -1)
    moved = [to_z(dense, j) for j in (1, 2, 3)]
    own, *others = [values] + [piece.reshape(values.shape) for piece in moved]
    low, high = (z & 1) != 0, (z & 2) != 0
    pairs = [
        jnp.concatenate([jnp.where(low, b, a), jnp.where(low, a, b)], axis=2)
        for a, b in ((own, others[0]), (others[1], others[2]))
    ]
    column = jnp.concatenate(
        [jnp.where(high, pairs[1], pairs[0]), jnp.where(high, pairs[0], pairs[1])], axis=2
    )
    other = swap(column.reshape(dense.shape[0], -1)).reshape(column.shape)
    whole = jnp.concatenate(
        [jnp.where(core != 0, other, column), jnp.where(core != 0, column, other)], axis=3
    )
    return whole, moved


def stat_gather(stat):
    if lax.axis_size("py") != 4 or lax.axis_size("px") != 2:
        return axis_gather(axis_gather(stat[None], "px", 0), "py", 0)
    pair = jnp.stack([stat, swap(stat)])
    return jnp.concatenate(
        [pair] + [lax.ppermute(pair, "py", xor_pairs("py", j)) for j in (1, 2, 3)], axis=0
    )


ANY = pl.BlockSpec(memory_space=pl.ANY)
WHOLE = pl.BlockSpec(memory_space=pltpu.VMEM)


def local(fsq_codes, in_weight, res_weight, up_weight, first_gain, second_gain):
    dims, frames, rows, cols = fsq_codes.shape
    channels = in_weight.shape[3]
    row_len = frames * COL
    res_taps, up_taps_own = tap_major(res_weight), paired_taps(up_weight)
    paired = tuple(lax.axis_size(axis) for axis in ("clip", "py", "px")) == (4, 4, 2)
    if paired:
        codes = code_gather(code_values(fsq_codes))
        res_part, up_part = column_part(res_taps), column_part(up_taps_own)
        res = [to_z(res_part, j) for j in (1, 2, 3)]
        res_other, up_other = (swap(after(own, codes[1])) for own in (res_taps, up_taps_own))
        waits = (res_other, up_other)
        act, feat, mark = prep(codes[0], in_weight, first_gain, rows, cols, waits)
        res_spread = to_clips(after(jnp.stack(res), mark))
        up = [to_z(after(up_part, mark, *res), j) for j in (2, 3)]
        up_near = to_z(after(up_taps_own, *res_spread), 1)
        up_spread = to_clips(after(jnp.stack(up), *res_spread))
        placed = [(res_taps, (), 0, None, 0), (res_other, (), 0, None, 1)]
        for d in range(4):
            for core, held in enumerate((res_spread[d], swap(res_spread[d]))):
                placed += [(held, (j - 1,), j, d, core) for j in (1, 2, 3)]
        res_sources, res_plan = placed_plan(placed)
    else:
        act, feat, _ = prep(code_gather(code_values(fsq_codes))[0], in_weight, first_gain, rows, cols)
        res_sources, res_plan = whole_gather(res_taps)
    hidden, stat = pl.pallas_call(
        lambda *refs: conv1_kernel(res_plan, rows, cols, *refs),
        out_shape=(
            jax.ShapeDtypeStruct(feat.shape, jnp.bfloat16),
            jax.ShapeDtypeStruct((8, channels), jnp.float32),
        ),
        in_specs=[ANY, ANY] + [ANY] * len(res_sources),
        scratch_shapes=[
            pltpu.VMEM((9, channels, channels), jnp.bfloat16),
            pltpu.VMEM(act.shape, jnp.bfloat16),
            pltpu.VMEM(feat.shape, jnp.bfloat16),
            pltpu.VMEM(feat.shape, jnp.float32),
            pltpu.SemaphoreType.DMA((9, 32)),
            pltpu.SemaphoreType.DMA((2,)),
        ],
        compiler_params=pltpu.CompilerParams(vmem_limit_bytes=VMEM_LIMIT),
        cost_estimate=pl.CostEstimate(
            flops=2 * 9 * feat.shape[0] * channels * channels, bytes_accessed=12 << 20, transcendentals=0
        ),
        name="conv1",
    )(act, feat, *res_sources)
    if paired:
        stat = after(stat, up_near, *up_spread)
        stats = stat_gather(stat)
        up_near, *up_spread = after((up_near, *up_spread), stat)
        placed = [(up_taps_own, (), 0, None, 0), (up_other, (), 0, None, 1)]
        placed += [(up_near, (), 1, None, 0), (swap(up_near), (), 1, None, 1)]
        for d in range(4):
            for core, held in enumerate((up_spread[d], swap(up_spread[d]))):
                placed += [(held, (j - 2,), j, d, core) for j in (2, 3)]
        up_sources, up_plan = placed_plan(placed)
    else:
        up_sources, up_plan = whole_gather(up_taps_own)
        stats = stat_gather(stat)
    py, px = lax.axis_index("py"), lax.axis_index("px")
    edges = jnp.stack(
        [py > 0, py < lax.axis_size("py") - 1, px > 0, px < lax.axis_size("px") - 1]
    ).astype(jnp.int32)
    step = 8
    return pl.pallas_call(
        lambda *refs: conv2_kernel(up_plan, rows, cols, *refs),
        out_shape=jax.ShapeDtypeStruct((frames, 2 * rows, 2 * cols, channels), jnp.bfloat16),
        in_specs=[pl.BlockSpec(memory_space=pltpu.SMEM), WHOLE, WHOLE, WHOLE]
        + [ANY] * len(up_sources),
        out_specs=ANY,
        scratch_shapes=[
            pltpu.VMEM((16, channels, channels), jnp.bfloat16),
            pltpu.VMEM((row_len, channels), jnp.float32),
            pltpu.VMEM(((rows + 2) * frames * cols, 3 * channels), jnp.bfloat16),
            pltpu.VMEM((2, channels // 128, 2 * step * frames * cols, 128), jnp.float32),
            pltpu.VMEM((frames, 2 * rows, 2 * cols, channels), jnp.bfloat16),
            pltpu.SemaphoreType.DMA((1, 32)),
            pltpu.SemaphoreType.DMA((rows // step, frames)),
        ],
        compiler_params=pltpu.CompilerParams(vmem_limit_bytes=VMEM_LIMIT),
        cost_estimate=pl.CostEstimate(
            flops=2 * 16 * frames * rows * cols * channels * channels,
            bytes_accessed=16 << 20,
            transcendentals=0,
        ),
        name="conv2",
    )(edges, hidden, stats, second_gain.reshape(1, channels), *up_sources)


def solution(mesh):
    placed = (
        P(None, "clip", "py", "px"),
        P(),
        P(("py", "px"), None, None, None),
        P(("py", "px"), None, None, None),
        P(),
        P(),
    )
    return jax.shard_map(
        local, mesh=mesh, in_specs=placed, out_specs=P("clip", "py", "px", None), check_vma=False
    )
```

```python
import jax
import jax.numpy as jnp
import numpy as np
from jax import lax
from jax.experimental import pallas as pl
from jax.experimental.pallas import tpu as pltpu
from jax.sharding import PartitionSpec as P

GROUPS = 32

fsq_levels = (8, 8, 8, 5, 5, 5)
epsilon = 1e-06
VMEM_LIMIT = 56 << 20
up_taps = (((1, 1), (3, 0)), ((0, 2), (2, 1)))

COL = 40


def axis_gather(cells, axis, dim):
    count = lax.axis_size(axis)
    me = lax.axis_index(axis)
    step = 1
    while step < count:
        other = lax.ppermute(cells, axis, [(i, i ^ step) for i in range(count)])
        upper = (me & step) != 0
        low = jnp.where(upper, other, cells)
        high = jnp.where(upper, cells, other)
        cells = jnp.concatenate([low, high], axis=dim)
        step *= 2
    return cells


def code_values(fsq_codes):
    levels = jnp.array(fsq_levels, jnp.int32).reshape(-1, 1, 1, 1)
    half_range = levels // 2
    values = (fsq_codes - half_range).astype(jnp.float32) / half_range.astype(jnp.float32)
    return values.astype(jnp.bfloat16)


def lanes_up(count):
    return (count + 127) // 128 * 128


def flat_inputs(values, rows, cols):
    dims, frames, height, width = values.shape
    py = lax.axis_index("py")
    px = lax.axis_index("px")
    clip = jnp.pad(values, ((0, 0), (0, 0), (1, 1), (1, 1)))
    inside = np.zeros((1, frames, height + 2, width + 2), np.float32)
    inside[:, :, :height, :width] = 1.0
    clip = jnp.concatenate([clip, jnp.asarray(inside, jnp.bfloat16), jnp.zeros_like(clip[:1])], axis=0)
    clip = clip.reshape(8, -1)
    clip = jnp.pad(clip, ((0, 0), (0, lanes_up(clip.shape[1]) - clip.shape[1])))

    wide = jnp.pad(values, ((0, 0), (0, 0), (3, 3), (3, 3)))
    patch = lax.dynamic_slice(
        wide, (0, 0, py * rows, px * cols), (dims, frames, rows + 6, cols + 6)
    )
    y = py * rows - 2 + jnp.arange(rows + 6)[:, None]
    x = px * cols - 2 + jnp.arange(cols + 6)[None, :]
    valid = (y >= 0) & (y < height) & (x >= 0) & (x < width)
    valid = jnp.broadcast_to(valid, (1, frames, rows + 6, cols + 6)).astype(jnp.bfloat16)
    patch = jnp.concatenate([patch, valid, jnp.zeros_like(valid)], axis=0)
    patch = jnp.pad(patch, ((0, 0), (0, 0), (0, 0), (0, COL - cols - 6)))
    patch = jnp.transpose(patch, (0, 2, 1, 3)).reshape(8, -1)
    return clip.astype(jnp.float32), patch.astype(jnp.float32)


def group_mean(row):
    lane = lax.broadcasted_iota(jnp.int32, row.shape, 1)
    width = row.shape[1]
    for step in (1, 2, 4, 8):
        row = row + jnp.where(
            (lane & step) != 0, pltpu.roll(row, step, 1), pltpu.roll(row, width - step, 1)
        )
    return row * (1.0 / 16.0)


def silu(t):
    return t * (0.5 * jnp.tanh(0.5 * t) + 0.5)


def tap_rows(flat, stride, keep=None):
    width = flat.shape[1]
    parts = []
    for tap in range(9):
        shift = (tap // 3) * stride + tap % 3
        part = flat if shift == 0 else pltpu.roll(flat, width - shift, 1)
        parts.append(part if keep is None else part * keep)
    parts.append(jnp.zeros_like(flat))
    return [
        jnp.concatenate(parts[2 * i : 2 * i + 2], axis=0).astype(jnp.bfloat16) for i in range(5)
    ]


def prep_kernel(clip_stride, clip_ref, w_ref, gain_ref, norm_ref, taps):
    channels = gain_ref.shape[1]
    for i, part in enumerate(tap_rows(clip_ref[...], clip_stride, clip_ref[6:7, :])):
        taps[16 * i : 16 * i + 16, :] = part
    moments = lax.dot_general(
        taps[...], taps[...], (((1,), (1,)), ((), ())), preferred_element_type=jnp.float32
    )
    total = moments[6:7, 6:7]
    mean_row = moments[6:7, :] / total
    mean_col = moments[:, 6:7] / total
    centred = moments / total - mean_col * mean_row
    weight32 = w_ref[:, :channels].astype(jnp.float32)
    spread_c = jnp.sum(
        weight32
        * jnp.dot(
            centred, weight32, precision=lax.Precision.HIGHEST, preferred_element_type=jnp.float32
        ),
        axis=0,
        keepdims=True,
    )
    mean_c = jnp.sum(weight32 * mean_col, axis=0, keepdims=True)
    mean_c = jnp.broadcast_to(mean_c, (8, channels))
    spread_c = jnp.broadcast_to(spread_c, (8, channels))
    average = group_mean(mean_c)
    apart = mean_c - average
    spread = jnp.maximum(group_mean(spread_c + apart * apart), 0.0)
    norm_ref[0:8, :] = average
    norm_ref[8:16, :] = lax.rsqrt(spread + epsilon) * gain_ref[...]


def features(patch, w_ref, norm_ref, wide, act, feat):
    channels = feat.shape[1]
    row_len = 2 * COL
    weight = w_ref[:, :channels]
    average = norm_ref[0:1, :]
    scale = norm_ref[8:9, :]
    span = patch.shape[1]
    window = jnp.concatenate(tap_rows(patch, row_len), axis=0)
    block = 256
    for start in range(0, span, block):
        size = min(block, span - start)
        product = lax.dot_general(
            window[:, start : start + size],
            w_ref[...],
            (((0,), (0,)), ((), ())),
            preferred_element_type=jnp.float32,
        )
        keep = product[:, channels : channels + 128]
        rounded = product[:, :channels].astype(jnp.bfloat16).astype(jnp.float32)
        active = silu((rounded - average) * scale)
        for lane in range(0, channels, 128):
            wide[start : start + size, lane : lane + 128] = active[:, lane : lane + 128] * keep
    count = act.shape[0]
    for shift in range(3):
        act[:, shift * channels : (shift + 1) * channels] = wide[shift : shift + count, :].astype(
            jnp.bfloat16
        )
    moved = pltpu.roll(patch, span - (row_len + 1), 1)
    window = jnp.concatenate(tap_rows(moved, row_len), axis=0)
    inner = feat.shape[0]
    for start in range(0, inner, block):
        size = min(block, inner - start)
        product = lax.dot_general(
            window[:, start : start + block],
            weight,
            (((0,), (0,)), ((), ())),
            preferred_element_type=jnp.float32,
        )
        feat[start : start + size, :] = product[:size].astype(jnp.bfloat16)


def prep(values, in_weight, gain, rows, cols, waits=()):
    channels = in_weight.shape[3]
    dims, frames, height, width = values.shape
    clip, patch = flat_inputs(values, rows, cols)
    span = patch.shape[1]
    pad = lanes_up(span + 2) - span
    patch = jnp.pad(patch, ((0, 0), (0, pad)))
    clip, patch = after((clip, patch), *waits)
    weight = jnp.pad(in_weight.reshape(9, dims, channels), ((0, 1), (0, 8 - dims), (0, 128)))
    marks = np.zeros((10, 8, channels + 128), np.float32)
    marks[0, 6, channels:] = 1.0
    weight = (weight + jnp.asarray(marks, jnp.bfloat16)).reshape(80, channels + 128)
    norm = pl.pallas_call(
        lambda *refs: prep_kernel(width + 2, *refs),
        out_shape=jax.ShapeDtypeStruct((16, channels), jnp.float32),
        scratch_shapes=[pltpu.VMEM((80, clip.shape[1]), jnp.bfloat16)],
        compiler_params=pltpu.CompilerParams(vmem_limit_bytes=(16 << 20) + 512 * clip.shape[1]),
        name="prep",
    )(clip, weight, gain.reshape(1, channels))
    return patch, weight, norm


def conv1_kernel(copy_plan, rows, cols, *refs):
    patch_ref, w_ref, norm_ref, *sources, hid_ref, stat_ref, weight, wide, act, feat, total, sems = refs
    row_len = 2 * COL
    copies = [copy_plan(sources, weight, sems, 3 * i, 3) for i in range(3)]
    for copy in copies[0] + copies[1] + copies[2]:
        copy.start()
    features(patch_ref[...], w_ref, norm_ref, wide, act, feat)
    channels = feat.shape[1]
    count = hid_ref.shape[0]
    group = count
    for row_tap in range(3):
        for copy in copies[row_tap]:
            copy.wait()
        taps = weight[3 * row_tap : 3 * row_tap + 3].reshape(3 * channels, channels)
        for start in range(0, count, group):
            size = min(group, count - start)
            first = start + row_tap * row_len
            product = jnp.dot(
                act[first : first + size, :], taps, preferred_element_type=jnp.float32
            )
            if row_tap == 0:
                total[start : start + size, :] = product + feat[start : start + size, :]
            elif row_tap == 1:
                total[start : start + size, :] += product
            else:
                hid_ref[start : start + size, :] = (total[start : start + size, :] + product).astype(
                    jnp.bfloat16
                )

    place = lax.broadcasted_iota(jnp.int32, (row_len, 128), 0)
    place = jnp.where(place >= COL, place - COL, place)
    keep = ((place >= 1) & (place <= cols)).astype(jnp.float32)
    keep = jnp.concatenate([keep] * (channels // 128), axis=1)
    lines = range(row_len, (rows + 1) * row_len, row_len)
    cells = 2.0 * rows * cols
    mean = jnp.zeros((row_len, channels), jnp.float32)
    for line in lines:
        mean = mean + hid_ref[line : line + row_len, :].astype(jnp.float32)
    mean = jnp.sum(mean * keep, axis=0, keepdims=True) / cells
    square = jnp.zeros((row_len, channels), jnp.float32)
    for line in lines:
        apart = hid_ref[line : line + row_len, :].astype(jnp.float32) - mean
        square = square + apart * apart
    stat_ref[0:1, :] = mean
    stat_ref[1:2, :] = jnp.sum(square * keep, axis=0, keepdims=True)
    stat_ref[2:8, :] = jnp.zeros((6, channels), jnp.float32)


def conv2_kernel(copy_plan, rows, cols, edge_ref, hid_ref, stat_ref, gain_ref, *refs):
    *sources, out_ref, weight, wide, shifted, woven, result, sems, out_sem = refs
    row_len = 2 * COL
    channels = hid_ref.shape[1]
    copies = copy_plan(sources, weight, sems, 0, 16)
    for copy in copies:
        copy.start()

    parts = stat_ref.shape[0]
    cells = 2.0 * rows * cols
    means = stat_ref[:, 0, :]
    average_c = jnp.sum(means, axis=0, keepdims=True) / parts
    apart = means - average_c
    square_c = jnp.sum(stat_ref[:, 1, :] + cells * apart * apart, axis=0, keepdims=True)
    average_c = jnp.broadcast_to(average_c, (8, channels))
    spread_c = jnp.broadcast_to(square_c, (8, channels)) / (cells * parts)
    average = group_mean(average_c)
    apart = average_c - average
    spread = group_mean(spread_c + apart * apart)
    scale = (lax.rsqrt(spread + epsilon) * gain_ref[...])[0:1, :]
    average = average[0:1, :]

    place = lax.broadcasted_iota(jnp.int32, (row_len, channels), 0)
    place = jnp.where(place >= COL, place - COL, place)
    top, bottom, left, right = (edge_ref[i].astype(jnp.float32) for i in range(4))
    keep = jnp.where(place == 0, left, jnp.where(place == cols + 1, right, 1.0))

    def normalise(line, _):
        first = pl.multiple_of(line * row_len, row_len)
        t = (hid_ref[pl.ds(first, row_len), :].astype(jnp.float32) - average) * scale
        row_keep = jnp.where(line == 0, top, jnp.where(line == rows + 1, bottom, 1.0))
        wide[...] = silu(t) * (keep * row_keep)
        for shift in range(3):
            for frame in range(2):
                to = pl.multiple_of(line * (2 * cols) + frame * cols, cols)
                shifted[pl.ds(to, cols), shift * channels : (shift + 1) * channels] = wide[
                    frame * COL + shift : frame * COL + shift + cols, :
                ].astype(jnp.bfloat16)
        return 0

    lax.fori_loop(0, rows + 2, normalise, 0)
    for copy in copies:
        copy.wait()

    step = 8
    size = step * 2 * cols

    for part in range(rows // step):
        line = part * step
        for row_phase in range(2):
            for col_phase in range(2):
                acc = None
                for row_kernel, row_offset in up_taps[row_phase]:
                    first = (line + row_offset) * (2 * cols)
                    tap = 4 * row_kernel + 2 * col_phase
                    product = jnp.dot(
                        shifted[
                            pl.ds(first, size), col_phase * channels : (col_phase + 2) * channels
                        ],
                        weight[tap : tap + 2].reshape(2 * channels, channels),
                        preferred_element_type=jnp.float32,
                    )
                    acc = product if acc is None else acc + product
                for lane in range(channels // 128):
                    woven[row_phase, lane, pl.ds(col_phase, size, stride=2), :] = acc[
                        :, 128 * lane : 128 * lane + 128
                    ]
            for y in range(step):
                for frame in range(2):
                    at = (2 * y + frame) * 2 * cols
                    for lane in range(channels // 128):
                        result[
                            frame,
                            2 * (line + y) + row_phase,
                            :,
                            128 * lane : 128 * lane + 128,
                        ] = woven[row_phase, lane, at : at + 2 * cols, :].astype(jnp.bfloat16)
        for frame in range(2):
            lines = pl.ds(2 * line, 2 * step)
            pltpu.make_async_copy(
                result.at[frame, lines], out_ref.at[frame, lines], out_sem.at[part, frame]
            ).start()
    for part in range(rows // step):
        for frame in range(2):
            lines = pl.ds(2 * step * part, 2 * step)
            pltpu.make_async_copy(
                result.at[frame, lines], out_ref.at[frame, lines], out_sem.at[part, frame]
            ).wait()


def xor_pairs(axis, bits):
    return [(i, i ^ bits) for i in range(lax.axis_size(axis))]


def tap_major(weight):
    return jnp.transpose(weight, (1, 2, 0, 3)).reshape(-1, weight.shape[0], weight.shape[3])


def paired_taps(weight):
    rows, _, _, width = weight.shape
    halves = weight.reshape(rows, 4, 2, 2, width)[:, :, ::-1, ::-1, :]
    return jnp.transpose(halves, (1, 3, 2, 0, 4)).reshape(16, rows, width)


def column_part(weight):
    width = weight.shape[2] // lax.axis_size("clip")
    return lax.dynamic_slice_in_dim(weight, lax.axis_index("clip") * width, width, axis=2)


def swap(piece):
    return lax.ppermute(piece, "px", xor_pairs("px", 1))


def whole_gather(weight):
    def plan(sources, weight, sems, first, taps):
        taps = pl.ds(first, taps)
        return [pltpu.make_async_copy(sources[0].at[taps], weight.at[taps], sems.at[first, 0])]

    return [lax.all_gather(weight, ("py", "px"), axis=1, tiled=True)], plan


def after(held, *waits):
    return lax.optimization_barrier((held, waits))[0]


def to_z(part, bits):
    return lax.ppermute(part, "py", xor_pairs("py", bits))


def to_clips(piece):
    return [piece] + [lax.ppermute(piece, "clip", xor_pairs("clip", d)) for d in (1, 2, 3)]


def both_cores(pieces):
    return [one for piece in pieces for one in (piece, swap(piece))]


def placed_plan(placed):
    sources = []
    for entry in placed:
        if not any(entry[0] is source for source in sources):
            sources.append(entry[0])
    slots = [next(i for i, source in enumerate(sources) if source is entry[0]) for entry in placed]

    def plan(refs, weight, sems, first, taps):
        core, z, clip = lax.axis_index("px"), lax.axis_index("py"), lax.axis_index("clip")
        taps = pl.ds(first, taps)
        copies = []
        for i, (slot, (_, lead, z_bits, clip_bits, core_bit)) in enumerate(zip(slots, placed)):
            ref = refs[slot]
            rows, width = ref.shape[-2:]
            row = pl.ds(pl.multiple_of((2 * (z ^ z_bits) + (core ^ core_bit)) * rows, rows), rows)
            if clip_bits is None:
                to = weight.at[taps, row, :]
            elif clip_bits >= 0:
                to = weight.at[
                    taps, row, pl.ds(pl.multiple_of((clip ^ clip_bits) * width, width), width)
                ]
            else:
                to = weight.at[taps, row, pl.ds(-(clip_bits + 1) * width, width)]
            copies.append(
                pltpu.make_async_copy(ref.at[(*lead, taps)], to, sems.at[first, i])
            )
        return copies

    return sources, plan


def code_gather(values):
    if lax.axis_size("py") != 4 or lax.axis_size("px") != 2:
        return axis_gather(axis_gather(values, "px", 3), "py", 2), values
    z, core = lax.axis_index("py"), lax.axis_index("px")
    dense = values.reshape(values.shape[0] * values.shape[1], -1)
    moved = [to_z(dense, j) for j in (1, 2, 3)]
    own, *others = [values] + [piece.reshape(values.shape) for piece in moved]
    low, high = (z & 1) != 0, (z & 2) != 0
    pairs = [
        jnp.concatenate([jnp.where(low, b, a), jnp.where(low, a, b)], axis=2)
        for a, b in ((own, others[0]), (others[1], others[2]))
    ]
    column = jnp.concatenate(
        [jnp.where(high, pairs[1], pairs[0]), jnp.where(high, pairs[0], pairs[1])], axis=2
    )
    other = swap(column.reshape(dense.shape[0], -1)).reshape(column.shape)
    whole = jnp.concatenate(
        [jnp.where(core != 0, other, column), jnp.where(core != 0, column, other)], axis=3
    )
    return whole, moved


def stat_gather(stat, other=None):
    if lax.axis_size("py") != 4 or lax.axis_size("px") != 2:
        return axis_gather(axis_gather(stat[None], "px", 0), "py", 0)
    pair = jnp.stack([stat, other])
    return jnp.concatenate(
        [pair] + [lax.ppermute(pair, "py", xor_pairs("py", j)) for j in (1, 2, 3)], axis=0
    )


ANY = pl.BlockSpec(memory_space=pl.ANY)
WHOLE = pl.BlockSpec(memory_space=pltpu.VMEM)


def local(fsq_codes, in_weight, res_weight, up_weight, first_gain, second_gain):
    dims, frames, rows, cols = fsq_codes.shape
    channels = in_weight.shape[3]
    row_len = frames * COL
    res_taps, up_taps_own = tap_major(res_weight), paired_taps(up_weight)
    paired = tuple(lax.axis_size(axis) for axis in ("clip", "py", "px")) == (4, 4, 2)
    if paired:
        codes = code_gather(code_values(fsq_codes))
        res_part, up_part = column_part(res_taps), column_part(up_taps_own)
        res = [to_z(res_part, j) for j in (1, 2, 3)]
        res_other, up_other = (swap(after(own, codes[1])) for own in (res_taps, up_taps_own))
        waits = (res_other, up_other)
        patch, in_taps, norm = prep(codes[0], in_weight, first_gain, rows, cols, waits)
        res_spread = to_clips(after(jnp.stack(res), norm))
        up = [to_z(after(up_part, norm, *res), 2)]
        up.append(to_z(up[0], 1))
        up_near = to_z(after(up_taps_own, *res_spread), 1)
        up_spread = to_clips(after(jnp.stack(up), *res_spread))
        placed = [(res_taps, (), 0, None, 0), (res_other, (), 0, None, 1)]
        for d in range(4):
            for core, held in enumerate((res_spread[d], swap(res_spread[d]))):
                placed += [(held, (j - 1,), j, d, core) for j in (1, 2, 3)]
        res_sources, res_plan = placed_plan(placed)
    else:
        patch, in_taps, norm = prep(code_gather(code_values(fsq_codes))[0], in_weight, first_gain, rows, cols)
        res_sources, res_plan = whole_gather(res_taps)
    cells = (rows + 2) * row_len
    hidden, stat = pl.pallas_call(
        lambda *refs: conv1_kernel(res_plan, rows, cols, *refs),
        out_shape=(
            jax.ShapeDtypeStruct((cells, channels), jnp.bfloat16),
            jax.ShapeDtypeStruct((8, channels), jnp.float32),
        ),
        in_specs=[WHOLE, WHOLE, WHOLE] + [ANY] * len(res_sources),
        scratch_shapes=[
            pltpu.VMEM((9, channels, channels), jnp.bfloat16),
            pltpu.VMEM((patch.shape[1], channels), jnp.float32),
            pltpu.VMEM((cells + 2 * row_len, 3 * channels), jnp.bfloat16),
            pltpu.VMEM((cells, channels), jnp.bfloat16),
            pltpu.VMEM((cells, channels), jnp.float32),
            pltpu.SemaphoreType.DMA((9, 32)),
        ],
        compiler_params=pltpu.CompilerParams(vmem_limit_bytes=VMEM_LIMIT),
        cost_estimate=pl.CostEstimate(
            flops=2 * 9 * cells * channels * channels, bytes_accessed=12 << 20, transcendentals=0
        ),
        name="conv1",
    )(patch, in_taps, norm, *res_sources)
    if paired:
        other = swap(stat)
        up_near, *up_spread = after((up_near, *up_spread), other)
        stats = stat_gather(stat, after(other, up_near, *up_spread))
        placed = [(up_taps_own, (), 0, None, 0), (up_other, (), 0, None, 1)]
        placed += [(up_near, (), 1, None, 0), (swap(up_near), (), 1, None, 1)]
        for d in range(4):
            for core, held in enumerate((up_spread[d], swap(up_spread[d]))):
                placed += [(held, (j - 2,), j, d, core) for j in (2, 3)]
        up_sources, up_plan = placed_plan(placed)
    else:
        up_sources, up_plan = whole_gather(up_taps_own)
        stats = stat_gather(stat)
    py, px = lax.axis_index("py"), lax.axis_index("px")
    edges = jnp.stack(
        [py > 0, py < lax.axis_size("py") - 1, px > 0, px < lax.axis_size("px") - 1]
    ).astype(jnp.int32)
    step = 8
    return pl.pallas_call(
        lambda *refs: conv2_kernel(up_plan, rows, cols, *refs),
        out_shape=jax.ShapeDtypeStruct((frames, 2 * rows, 2 * cols, channels), jnp.bfloat16),
        in_specs=[pl.BlockSpec(memory_space=pltpu.SMEM), WHOLE, WHOLE, WHOLE]
        + [ANY] * len(up_sources),
        out_specs=ANY,
        scratch_shapes=[
            pltpu.VMEM((16, channels, channels), jnp.bfloat16),
            pltpu.VMEM((row_len, channels), jnp.float32),
            pltpu.VMEM(((rows + 2) * frames * cols, 3 * channels), jnp.bfloat16),
            pltpu.VMEM((2, channels // 128, 2 * step * frames * cols, 128), jnp.float32),
            pltpu.VMEM((frames, 2 * rows, 2 * cols, channels), jnp.bfloat16),
            pltpu.SemaphoreType.DMA((1, 32)),
            pltpu.SemaphoreType.DMA((rows // step, frames)),
        ],
        compiler_params=pltpu.CompilerParams(vmem_limit_bytes=VMEM_LIMIT),
        cost_estimate=pl.CostEstimate(
            flops=2 * 16 * frames * rows * cols * channels * channels,
            bytes_accessed=16 << 20,
            transcendentals=0,
        ),
        name="conv2",
    )(edges, hidden, stats, second_gain.reshape(1, channels), *up_sources)


def solution(mesh):
    placed = (
        P(None, "clip", "py", "px"),
        P(),
        P(("py", "px"), None, None, None),
        P(("py", "px"), None, None, None),
        P(),
        P(),
    )
    return jax.shard_map(
        local, mesh=mesh, in_specs=placed, out_specs=P("clip", "py", "px", None), check_vma=False
    )
```

```python
import jax
import jax.numpy as jnp
import numpy as np
from jax import lax
from jax.experimental import pallas as pl
from jax.experimental.pallas import tpu as pltpu
from jax.sharding import PartitionSpec as P

GROUPS = 32

fsq_levels = (8, 8, 8, 5, 5, 5)
epsilon = 1e-06
VMEM_LIMIT = 56 << 20
up_taps = (((1, 1), (3, 0)), ((0, 2), (2, 1)))

COL = 40


def axis_gather(cells, axis, dim):
    count = lax.axis_size(axis)
    me = lax.axis_index(axis)
    step = 1
    while step < count:
        other = lax.ppermute(cells, axis, [(i, i ^ step) for i in range(count)])
        upper = (me & step) != 0
        low = jnp.where(upper, other, cells)
        high = jnp.where(upper, cells, other)
        cells = jnp.concatenate([low, high], axis=dim)
        step *= 2
    return cells


def code_values(fsq_codes):
    levels = jnp.array(fsq_levels, jnp.int32).reshape(-1, 1, 1, 1)
    half_range = levels // 2
    values = (fsq_codes - half_range).astype(jnp.float32) / half_range.astype(jnp.float32)
    return values.astype(jnp.bfloat16)


def lanes_up(count):
    return (count + 127) // 128 * 128


def flat_inputs(values, rows, cols):
    dims, frames, height, width = values.shape
    py = lax.axis_index("py")
    px = lax.axis_index("px")
    clip = jnp.pad(values, ((0, 0), (0, 0), (1, 1), (1, 1)))
    inside = np.zeros((1, frames, height + 2, width + 2), np.float32)
    inside[:, :, :height, :width] = 1.0
    clip = jnp.concatenate([clip, jnp.asarray(inside, jnp.bfloat16), jnp.zeros_like(clip[:1])], axis=0)
    clip = clip.reshape(8, -1)
    clip = jnp.pad(clip, ((0, 0), (0, lanes_up(clip.shape[1]) - clip.shape[1])))

    wide = jnp.pad(values, ((0, 0), (0, 0), (3, 3), (3, 3)))
    patch = lax.dynamic_slice(
        wide, (0, 0, py * rows, px * cols), (dims, frames, rows + 6, cols + 6)
    )
    y = py * rows - 2 + jnp.arange(rows + 6)[:, None]
    x = px * cols - 2 + jnp.arange(cols + 6)[None, :]
    valid = (y >= 0) & (y < height) & (x >= 0) & (x < width)
    valid = jnp.broadcast_to(valid, (1, frames, rows + 6, cols + 6)).astype(jnp.bfloat16)
    patch = jnp.concatenate([patch, valid, jnp.zeros_like(valid)], axis=0)
    patch = jnp.pad(patch, ((0, 0), (0, 0), (0, 0), (0, COL - cols - 6)))
    patch = jnp.transpose(patch, (0, 2, 1, 3)).reshape(8, -1)
    return clip.astype(jnp.float32), patch.astype(jnp.float32)


def group_mean(row):
    lane = lax.broadcasted_iota(jnp.int32, row.shape, 1)
    width = row.shape[1]
    for step in (1, 2, 4, 8):
        row = row + jnp.where(
            (lane & step) != 0, pltpu.roll(row, step, 1), pltpu.roll(row, width - step, 1)
        )
    return row * (1.0 / 16.0)


def silu(t):
    return t * (0.5 * jnp.tanh(0.5 * t) + 0.5)


def tap_rows(flat, stride, keep=None):
    width = flat.shape[1]
    parts = []
    for tap in range(9):
        shift = (tap // 3) * stride + tap % 3
        part = flat if shift == 0 else pltpu.roll(flat, width - shift, 1)
        parts.append(part if keep is None else part * keep)
    parts.append(jnp.zeros_like(flat))
    return [
        jnp.concatenate(parts[2 * i : 2 * i + 2], axis=0).astype(jnp.bfloat16) for i in range(5)
    ]


def prep_kernel(clip_stride, clip_ref, w_ref, gain_ref, norm_ref, taps):
    channels = gain_ref.shape[1]
    for i, part in enumerate(tap_rows(clip_ref[...], clip_stride, clip_ref[6:7, :])):
        taps[16 * i : 16 * i + 16, :] = part
    moments = lax.dot_general(
        taps[...], taps[...], (((1,), (1,)), ((), ())), preferred_element_type=jnp.float32
    )
    total = moments[6:7, 6:7]
    mean_row = moments[6:7, :] / total
    mean_col = moments[:, 6:7] / total
    centred = moments / total - mean_col * mean_row
    weight32 = w_ref[:, :channels].astype(jnp.float32)
    spread_c = jnp.sum(
        weight32
        * jnp.dot(
            centred, weight32, precision=lax.Precision.HIGHEST, preferred_element_type=jnp.float32
        ),
        axis=0,
        keepdims=True,
    )
    mean_c = jnp.sum(weight32 * mean_col, axis=0, keepdims=True)
    mean_c = jnp.broadcast_to(mean_c, (8, channels))
    spread_c = jnp.broadcast_to(spread_c, (8, channels))
    average = group_mean(mean_c)
    apart = mean_c - average
    spread = jnp.maximum(group_mean(spread_c + apart * apart), 0.0)
    norm_ref[0:8, :] = average
    norm_ref[8:16, :] = lax.rsqrt(spread + epsilon) * gain_ref[...]


def features(patch, w_ref, norm_ref, wide, act, feat):
    channels = feat.shape[1]
    row_len = 2 * COL
    weight = w_ref[:, :channels]
    average = norm_ref[0:1, :]
    scale = norm_ref[8:9, :]
    span = patch.shape[1]
    window = jnp.concatenate(tap_rows(patch, row_len), axis=0)
    block = 256
    for start in range(0, span, block):
        size = min(block, span - start)
        product = lax.dot_general(
            window[:, start : start + size],
            w_ref[...],
            (((0,), (0,)), ((), ())),
            preferred_element_type=jnp.float32,
        )
        keep = product[:, channels : channels + 128]
        rounded = product[:, :channels].astype(jnp.bfloat16).astype(jnp.float32)
        active = silu((rounded - average) * scale)
        for lane in range(0, channels, 128):
            wide[start : start + size, lane : lane + 128] = active[:, lane : lane + 128] * keep
    count = act.shape[0]
    for shift in range(3):
        act[:, shift * channels : (shift + 1) * channels] = wide[shift : shift + count, :].astype(
            jnp.bfloat16
        )
    moved = pltpu.roll(patch, span - (row_len + 1), 1)
    window = jnp.concatenate(tap_rows(moved, row_len), axis=0)
    inner = feat.shape[0]
    for start in range(0, inner, block):
        size = min(block, inner - start)
        product = lax.dot_general(
            window[:, start : start + block],
            weight,
            (((0,), (0,)), ((), ())),
            preferred_element_type=jnp.float32,
        )
        feat[start : start + size, :] = product[:size].astype(jnp.bfloat16)


def prep(values, in_weight, gain, rows, cols, waits=()):
    channels = in_weight.shape[3]
    dims, frames, height, width = values.shape
    clip, patch = flat_inputs(values, rows, cols)
    span = patch.shape[1]
    pad = lanes_up(span + 2) - span
    patch = jnp.pad(patch, ((0, 0), (0, pad)))
    clip, patch = after((clip, patch), *waits)
    weight = jnp.pad(in_weight.reshape(9, dims, channels), ((0, 1), (0, 8 - dims), (0, 128)))
    marks = np.zeros((10, 8, channels + 128), np.float32)
    marks[0, 6, channels:] = 1.0
    weight = (weight + jnp.asarray(marks, jnp.bfloat16)).reshape(80, channels + 128)
    norm = pl.pallas_call(
        lambda *refs: prep_kernel(width + 2, *refs),
        out_shape=jax.ShapeDtypeStruct((16, channels), jnp.float32),
        scratch_shapes=[pltpu.VMEM((80, clip.shape[1]), jnp.bfloat16)],
        compiler_params=pltpu.CompilerParams(vmem_limit_bytes=(16 << 20) + 512 * clip.shape[1]),
        name="prep",
    )(clip, weight, gain.reshape(1, channels))
    return patch, weight, norm


def conv1_kernel(copy_plan, rows, cols, *refs):
    patch_ref, w_ref, norm_ref, *sources, hid_ref, stat_ref, weight, wide, act, feat, total, sems = refs
    row_len = 2 * COL
    copies = [copy_plan(sources, weight, sems, 3 * i, 3) for i in range(3)]
    for copy in copies[0] + copies[1] + copies[2]:
        copy.start()
    features(patch_ref[...], w_ref, norm_ref, wide, act, feat)
    channels = feat.shape[1]
    count = hid_ref.shape[0]
    group = count
    for row_tap in range(3):
        for copy in copies[row_tap]:
            copy.wait()
        taps = weight[3 * row_tap : 3 * row_tap + 3].reshape(3 * channels, channels)
        for start in range(0, count, group):
            size = min(group, count - start)
            first = start + row_tap * row_len
            product = jnp.dot(
                act[first : first + size, :], taps, preferred_element_type=jnp.float32
            )
            if row_tap == 0:
                total[start : start + size, :] = product + feat[start : start + size, :]
            elif row_tap == 1:
                total[start : start + size, :] += product
            else:
                hid_ref[start : start + size, :] = (total[start : start + size, :] + product).astype(
                    jnp.bfloat16
                )

    place = lax.broadcasted_iota(jnp.int32, (row_len, 128), 0)
    place = jnp.where(place >= COL, place - COL, place)
    keep = ((place >= 1) & (place <= cols)).astype(jnp.float32)
    keep = jnp.concatenate([keep] * (channels // 128), axis=1)
    lines = range(row_len, (rows + 1) * row_len, row_len)
    cells = 2.0 * rows * cols
    mean = jnp.zeros((row_len, channels), jnp.float32)
    for line in lines:
        mean = mean + hid_ref[line : line + row_len, :].astype(jnp.float32)
    mean = jnp.sum(mean * keep, axis=0, keepdims=True) / cells
    square = jnp.zeros((row_len, channels), jnp.float32)
    for line in lines:
        apart = hid_ref[line : line + row_len, :].astype(jnp.float32) - mean
        square = square + apart * apart
    stat_ref[0:1, :] = mean
    stat_ref[1:2, :] = jnp.sum(square * keep, axis=0, keepdims=True)
    stat_ref[2:8, :] = jnp.zeros((6, channels), jnp.float32)


def conv2_kernel(copy_plan, rows, cols, edge_ref, hid_ref, stat_ref, gain_ref, *refs):
    *sources, out_ref, weight, wide, shifted, woven, result, sems, out_sem = refs
    row_len = 2 * COL
    channels = hid_ref.shape[1]
    copies = [copy_plan(sources, weight, sems, 4 * i, 4) for i in range(4)]
    for copy in copies[0] + copies[1]:
        copy.start()

    parts = stat_ref.shape[0]
    cells = 2.0 * rows * cols
    means = stat_ref[:, 0, :]
    average_c = jnp.sum(means, axis=0, keepdims=True) / parts
    apart = means - average_c
    square_c = jnp.sum(stat_ref[:, 1, :] + cells * apart * apart, axis=0, keepdims=True)
    average_c = jnp.broadcast_to(average_c, (8, channels))
    spread_c = jnp.broadcast_to(square_c, (8, channels)) / (cells * parts)
    average = group_mean(average_c)
    apart = average_c - average
    spread = group_mean(spread_c + apart * apart)
    scale = (lax.rsqrt(spread + epsilon) * gain_ref[...])[0:1, :]
    average = average[0:1, :]

    place = lax.broadcasted_iota(jnp.int32, (row_len, channels), 0)
    place = jnp.where(place >= COL, place - COL, place)
    top, bottom, left, right = (edge_ref[i].astype(jnp.float32) for i in range(4))
    keep = jnp.where(place == 0, left, jnp.where(place == cols + 1, right, 1.0))

    def normalise(line, _):
        first = pl.multiple_of(line * row_len, row_len)
        t = (hid_ref[pl.ds(first, row_len), :].astype(jnp.float32) - average) * scale
        row_keep = jnp.where(line == 0, top, jnp.where(line == rows + 1, bottom, 1.0))
        wide[...] = silu(t) * (keep * row_keep)
        for shift in range(3):
            for frame in range(2):
                to = pl.multiple_of(line * (2 * cols) + frame * cols, cols)
                shifted[pl.ds(to, cols), shift * channels : (shift + 1) * channels] = wide[
                    frame * COL + shift : frame * COL + shift + cols, :
                ].astype(jnp.bfloat16)
        return 0

    lax.fori_loop(0, rows + 2, normalise, 0)

    step = 8
    parts = rows // step
    size = step * 2 * cols

    def out_copy(part, row_phase):
        lines = pl.ds(part * step, step)
        return pltpu.make_async_copy(
            result.at[:, lines, row_phase],
            out_ref.at[:, lines, row_phase],
            out_sem.at[part, row_phase],
        )

    for row_phase in range(2):
        for col_phase in range(2):
            phase = 2 * row_phase + col_phase
            for copy in copies[phase]:
                copy.wait()
            if phase < 2:
                for copy in copies[phase + 2]:
                    copy.start()
            for part in range(parts):
                acc = None
                for i, (_, row_offset) in enumerate(up_taps[row_phase]):
                    first = (part * step + row_offset) * (2 * cols)
                    tap = 4 * phase + 2 * i
                    product = jnp.dot(
                        shifted[
                            first : first + size, col_phase * channels : (col_phase + 2) * channels
                        ],
                        weight[tap : tap + 2].reshape(2 * channels, channels),
                        preferred_element_type=jnp.float32,
                    )
                    acc = product if acc is None else acc + product
                for lane in range(channels // 128):
                    woven[part, lane, pl.ds(col_phase, size, stride=2), :] = acc[
                        :, 128 * lane : 128 * lane + 128
                    ]
                if col_phase == 0:
                    continue
                for y in range(step):
                    for frame in range(2):
                        at = (2 * y + frame) * 2 * cols
                        for lane in range(channels // 128):
                            result[
                                frame, part * step + y, row_phase, :, 128 * lane : 128 * lane + 128
                            ] = woven[part, lane, at : at + 2 * cols, :].astype(jnp.bfloat16)
                out_copy(part, row_phase).start()
    for row_phase in range(2):
        for part in range(parts):
            out_copy(part, row_phase).wait()


def xor_pairs(axis, bits):
    return [(i, i ^ bits) for i in range(lax.axis_size(axis))]


def tap_major(weight):
    return jnp.transpose(weight, (1, 2, 0, 3)).reshape(-1, weight.shape[0], weight.shape[3])


def paired_taps(weight):
    rows, _, _, width = weight.shape
    halves = weight.reshape(rows, 2, 2, 2, 2, width)[:, :, ::-1, ::-1, ::-1, :]
    return jnp.transpose(halves, (2, 4, 1, 3, 0, 5)).reshape(16, rows, width)


def column_part(weight):
    width = weight.shape[2] // lax.axis_size("clip")
    return lax.dynamic_slice_in_dim(weight, lax.axis_index("clip") * width, width, axis=2)


def swap(piece):
    return lax.ppermute(piece, "px", xor_pairs("px", 1))


def whole_gather(weight):
    def plan(sources, weight, sems, first, taps):
        taps = pl.ds(first, taps)
        return [pltpu.make_async_copy(sources[0].at[taps], weight.at[taps], sems.at[first, 0])]

    return [lax.all_gather(weight, ("py", "px"), axis=1, tiled=True)], plan


def after(held, *waits):
    return lax.optimization_barrier((held, waits))[0]


def to_z(part, bits):
    return lax.ppermute(part, "py", xor_pairs("py", bits))


def to_clips(piece):
    return [piece] + [lax.ppermute(piece, "clip", xor_pairs("clip", d)) for d in (1, 2, 3)]


def both_cores(pieces):
    return [one for piece in pieces for one in (piece, swap(piece))]


def placed_plan(placed):
    sources = []
    for entry in placed:
        if not any(entry[0] is source for source in sources):
            sources.append(entry[0])
    slots = [next(i for i, source in enumerate(sources) if source is entry[0]) for entry in placed]

    def plan(refs, weight, sems, first, taps):
        core, z, clip = lax.axis_index("px"), lax.axis_index("py"), lax.axis_index("clip")
        taps = pl.ds(first, taps)
        copies = []
        for i, (slot, (_, lead, z_bits, clip_bits, core_bit)) in enumerate(zip(slots, placed)):
            ref = refs[slot]
            rows, width = ref.shape[-2:]
            row = pl.ds(pl.multiple_of((2 * (z ^ z_bits) + (core ^ core_bit)) * rows, rows), rows)
            if clip_bits is None:
                to = weight.at[taps, row, :]
            elif clip_bits >= 0:
                to = weight.at[
                    taps, row, pl.ds(pl.multiple_of((clip ^ clip_bits) * width, width), width)
                ]
            else:
                to = weight.at[taps, row, pl.ds(-(clip_bits + 1) * width, width)]
            copies.append(
                pltpu.make_async_copy(ref.at[(*lead, taps)], to, sems.at[first, i])
            )
        return copies

    return sources, plan


def code_gather(values):
    if lax.axis_size("py") != 4 or lax.axis_size("px") != 2:
        return axis_gather(axis_gather(values, "px", 3), "py", 2), values
    z, core = lax.axis_index("py"), lax.axis_index("px")
    dense = values.reshape(values.shape[0] * values.shape[1], -1)
    moved = [to_z(dense, j) for j in (1, 2, 3)]
    own, *others = [values] + [piece.reshape(values.shape) for piece in moved]
    low, high = (z & 1) != 0, (z & 2) != 0
    pairs = [
        jnp.concatenate([jnp.where(low, b, a), jnp.where(low, a, b)], axis=2)
        for a, b in ((own, others[0]), (others[1], others[2]))
    ]
    column = jnp.concatenate(
        [jnp.where(high, pairs[1], pairs[0]), jnp.where(high, pairs[0], pairs[1])], axis=2
    )
    other = swap(column.reshape(dense.shape[0], -1)).reshape(column.shape)
    whole = jnp.concatenate(
        [jnp.where(core != 0, other, column), jnp.where(core != 0, column, other)], axis=3
    )
    return whole, moved


def stat_gather(stat, other=None):
    if lax.axis_size("py") != 4 or lax.axis_size("px") != 2:
        return axis_gather(axis_gather(stat[None], "px", 0), "py", 0)
    pair = jnp.stack([stat, other])
    return jnp.concatenate(
        [pair] + [lax.ppermute(pair, "py", xor_pairs("py", j)) for j in (1, 2, 3)], axis=0
    )


ANY = pl.BlockSpec(memory_space=pl.ANY)
WHOLE = pl.BlockSpec(memory_space=pltpu.VMEM)


def local(fsq_codes, in_weight, res_weight, up_weight, first_gain, second_gain):
    dims, frames, rows, cols = fsq_codes.shape
    channels = in_weight.shape[3]
    row_len = frames * COL
    res_taps, up_taps_own = tap_major(res_weight), paired_taps(up_weight)
    paired = tuple(lax.axis_size(axis) for axis in ("clip", "py", "px")) == (4, 4, 2)
    if paired:
        codes = code_gather(code_values(fsq_codes))
        res_part, up_part = column_part(res_taps), column_part(up_taps_own)
        res = [to_z(res_part, j) for j in (1, 2, 3)]
        res_other, up_other = (swap(after(own, codes[1])) for own in (res_taps, up_taps_own))
        waits = (res_other, up_other)
        patch, in_taps, norm = prep(codes[0], in_weight, first_gain, rows, cols, waits)
        res_spread = to_clips(after(jnp.stack(res), norm))
        up = [to_z(after(up_part, norm, *res), 2)]
        up.append(to_z(up[0], 1))
        up_near = to_z(after(up_taps_own, *res_spread), 1)
        up_spread = to_clips(after(jnp.stack(up), *res_spread))
        placed = [(res_taps, (), 0, None, 0), (res_other, (), 0, None, 1)]
        for d in range(4):
            for core, held in enumerate((res_spread[d], swap(res_spread[d]))):
                placed += [(held, (j - 1,), j, d, core) for j in (1, 2, 3)]
        res_sources, res_plan = placed_plan(placed)
    else:
        patch, in_taps, norm = prep(code_gather(code_values(fsq_codes))[0], in_weight, first_gain, rows, cols)
        res_sources, res_plan = whole_gather(res_taps)
    cells = (rows + 2) * row_len
    hidden, stat = pl.pallas_call(
        lambda *refs: conv1_kernel(res_plan, rows, cols, *refs),
        out_shape=(
            jax.ShapeDtypeStruct((cells, channels), jnp.bfloat16),
            jax.ShapeDtypeStruct((8, channels), jnp.float32),
        ),
        in_specs=[WHOLE, WHOLE, WHOLE] + [ANY] * len(res_sources),
        scratch_shapes=[
            pltpu.VMEM((9, channels, channels), jnp.bfloat16),
            pltpu.VMEM((patch.shape[1], channels), jnp.float32),
            pltpu.VMEM((cells + 2 * row_len, 3 * channels), jnp.bfloat16),
            pltpu.VMEM((cells, channels), jnp.bfloat16),
            pltpu.VMEM((cells, channels), jnp.float32),
            pltpu.SemaphoreType.DMA((9, 32)),
        ],
        compiler_params=pltpu.CompilerParams(vmem_limit_bytes=VMEM_LIMIT),
        cost_estimate=pl.CostEstimate(
            flops=2 * 9 * cells * channels * channels, bytes_accessed=12 << 20, transcendentals=0
        ),
        name="conv1",
    )(patch, in_taps, norm, *res_sources)
    if paired:
        other = swap(stat)
        up_near, *up_spread = after((up_near, *up_spread), other)
        stats = stat_gather(stat, after(other, up_near, *up_spread))
        placed = [(up_taps_own, (), 0, None, 0), (up_other, (), 0, None, 1)]
        placed += [(up_near, (), 1, None, 0), (swap(up_near), (), 1, None, 1)]
        for d in range(4):
            for core, held in enumerate((up_spread[d], swap(up_spread[d]))):
                placed += [(held, (j - 2,), j, d, core) for j in (2, 3)]
        up_sources, up_plan = placed_plan(placed)
    else:
        up_sources, up_plan = whole_gather(up_taps_own)
        stats = stat_gather(stat)
    py, px = lax.axis_index("py"), lax.axis_index("px")
    edges = jnp.stack(
        [py > 0, py < lax.axis_size("py") - 1, px > 0, px < lax.axis_size("px") - 1]
    ).astype(jnp.int32)
    step = 8
    return pl.pallas_call(
        lambda *refs: conv2_kernel(up_plan, rows, cols, *refs),
        out_shape=jax.ShapeDtypeStruct((frames, rows, 2, 2 * cols, channels), jnp.bfloat16),
        in_specs=[pl.BlockSpec(memory_space=pltpu.SMEM), WHOLE, WHOLE, WHOLE]
        + [ANY] * len(up_sources),
        out_specs=ANY,
        scratch_shapes=[
            pltpu.VMEM((16, channels, channels), jnp.bfloat16),
            pltpu.VMEM((row_len, channels), jnp.float32),
            pltpu.VMEM(((rows + 2) * frames * cols, 3 * channels), jnp.bfloat16),
            pltpu.VMEM((rows // step, channels // 128, 2 * step * frames * cols, 128), jnp.float32),
            pltpu.VMEM((frames, rows, 2, 2 * cols, channels), jnp.bfloat16),
            pltpu.SemaphoreType.DMA((16, 32)),
            pltpu.SemaphoreType.DMA((rows // step, 2)),
        ],
        compiler_params=pltpu.CompilerParams(vmem_limit_bytes=VMEM_LIMIT),
        cost_estimate=pl.CostEstimate(
            flops=2 * 16 * frames * rows * cols * channels * channels,
            bytes_accessed=16 << 20,
            transcendentals=0,
        ),
        name="conv2",
    )(edges, hidden, stats, second_gain.reshape(1, channels), *up_sources).reshape(frames, 2 * rows, 2 * cols, channels)


def solution(mesh):
    placed = (
        P(None, "clip", "py", "px"),
        P(),
        P(("py", "px"), None, None, None),
        P(("py", "px"), None, None, None),
        P(),
        P(),
    )
    return jax.shard_map(
        local, mesh=mesh, in_specs=placed, out_specs=P("clip", "py", "px", None), check_vma=False
    )
```

```python
import jax
import jax.numpy as jnp
import numpy as np
from jax import lax
from jax.experimental import pallas as pl
from jax.experimental.pallas import tpu as pltpu
from jax.sharding import PartitionSpec as P

GROUPS = 32

fsq_levels = (8, 8, 8, 5, 5, 5)
epsilon = 1e-06
VMEM_LIMIT = 56 << 20
up_taps = (((1, 1), (3, 0)), ((0, 2), (2, 1)))

COL = 40


def axis_gather(cells, axis, dim):
    count = lax.axis_size(axis)
    me = lax.axis_index(axis)
    step = 1
    while step < count:
        other = lax.ppermute(cells, axis, [(i, i ^ step) for i in range(count)])
        upper = (me & step) != 0
        low = jnp.where(upper, other, cells)
        high = jnp.where(upper, cells, other)
        cells = jnp.concatenate([low, high], axis=dim)
        step *= 2
    return cells


def code_values(fsq_codes):
    levels = jnp.array(fsq_levels, jnp.int32).reshape(-1, 1, 1, 1)
    half_range = levels // 2
    values = (fsq_codes - half_range).astype(jnp.float32) / half_range.astype(jnp.float32)
    return values.astype(jnp.bfloat16)


def lanes_up(count):
    return (count + 127) // 128 * 128


def flat_inputs(values, rows, cols):
    dims, frames, height, width = values.shape
    py = lax.axis_index("py")
    px = lax.axis_index("px")
    clip = jnp.pad(values, ((0, 0), (0, 0), (1, 1), (1, 1)))
    inside = np.zeros((1, frames, height + 2, width + 2), np.float32)
    inside[:, :, :height, :width] = 1.0
    clip = jnp.concatenate([clip, jnp.asarray(inside, jnp.bfloat16), jnp.zeros_like(clip[:1])], axis=0)
    clip = clip.reshape(8, -1)
    clip = jnp.pad(clip, ((0, 0), (0, lanes_up(clip.shape[1]) - clip.shape[1])))

    wide = jnp.pad(values, ((0, 0), (0, 0), (3, 3), (3, 3)))
    patch = lax.dynamic_slice(
        wide, (0, 0, py * rows, px * cols), (dims, frames, rows + 6, cols + 6)
    )
    y = py * rows - 2 + jnp.arange(rows + 6)[:, None]
    x = px * cols - 2 + jnp.arange(cols + 6)[None, :]
    valid = (y >= 0) & (y < height) & (x >= 0) & (x < width)
    valid = jnp.broadcast_to(valid, (1, frames, rows + 6, cols + 6)).astype(jnp.bfloat16)
    patch = jnp.concatenate([patch, valid, jnp.zeros_like(valid)], axis=0)
    patch = jnp.pad(patch, ((0, 0), (0, 0), (0, 0), (0, COL - cols - 6)))
    patch = jnp.transpose(patch, (0, 2, 1, 3)).reshape(8, -1)
    return clip.astype(jnp.float32), patch.astype(jnp.float32)


def group_mean(row):
    lane = lax.broadcasted_iota(jnp.int32, row.shape, 1)
    width = row.shape[1]
    for step in (1, 2, 4, 8):
        row = row + jnp.where(
            (lane & step) != 0, pltpu.roll(row, step, 1), pltpu.roll(row, width - step, 1)
        )
    return row * (1.0 / 16.0)


def silu(t):
    return t * (0.5 * jnp.tanh(0.5 * t) + 0.5)


def tap_rows(flat, stride, keep=None):
    width = flat.shape[1]
    parts = []
    for tap in range(9):
        shift = (tap // 3) * stride + tap % 3
        part = flat if shift == 0 else pltpu.roll(flat, width - shift, 1)
        parts.append(part if keep is None else part * keep)
    parts.append(jnp.zeros_like(flat))
    return [
        jnp.concatenate(parts[2 * i : 2 * i + 2], axis=0).astype(jnp.bfloat16) for i in range(5)
    ]


def prep_kernel(clip_stride, clip_ref, w_ref, gain_ref, norm_ref, taps):
    channels = gain_ref.shape[1]
    for i, part in enumerate(tap_rows(clip_ref[...], clip_stride, clip_ref[6:7, :])):
        taps[16 * i : 16 * i + 16, :] = part
    moments = lax.dot_general(
        taps[...], taps[...], (((1,), (1,)), ((), ())), preferred_element_type=jnp.float32
    )
    total = moments[6:7, 6:7]
    mean_row = moments[6:7, :] / total
    mean_col = moments[:, 6:7] / total
    centred = moments / total - mean_col * mean_row
    weight32 = w_ref[:, :channels].astype(jnp.float32)
    spread_c = jnp.sum(
        weight32
        * jnp.dot(
            centred, weight32, precision=lax.Precision.HIGHEST, preferred_element_type=jnp.float32
        ),
        axis=0,
        keepdims=True,
    )
    mean_c = jnp.sum(weight32 * mean_col, axis=0, keepdims=True)
    mean_c = jnp.broadcast_to(mean_c, (8, channels))
    spread_c = jnp.broadcast_to(spread_c, (8, channels))
    average = group_mean(mean_c)
    apart = mean_c - average
    spread = jnp.maximum(group_mean(spread_c + apart * apart), 0.0)
    norm_ref[0:8, :] = average
    norm_ref[8:16, :] = lax.rsqrt(spread + epsilon) * gain_ref[...]


def features(patch, w_ref, norm_ref, wide, act, feat):
    channels = feat.shape[1]
    row_len = 2 * COL
    weight = w_ref[:, :channels]
    average = norm_ref[0:1, :]
    scale = norm_ref[8:9, :]
    span = patch.shape[1]
    window = jnp.concatenate(tap_rows(patch, row_len), axis=0)
    block = 256
    for start in range(0, span, block):
        size = min(block, span - start)
        product = lax.dot_general(
            window[:, start : start + size],
            w_ref[...],
            (((0,), (0,)), ((), ())),
            preferred_element_type=jnp.float32,
        )
        keep = product[:, channels : channels + 128]
        rounded = product[:, :channels].astype(jnp.bfloat16).astype(jnp.float32)
        active = silu((rounded - average) * scale)
        for lane in range(0, channels, 128):
            wide[start : start + size, lane : lane + 128] = active[:, lane : lane + 128] * keep
    count = act.shape[0]
    for shift in range(3):
        act[:, shift * channels : (shift + 1) * channels] = wide[shift : shift + count, :].astype(
            jnp.bfloat16
        )
    moved = pltpu.roll(patch, span - (row_len + 1), 1)
    window = jnp.concatenate(tap_rows(moved, row_len), axis=0)
    inner = feat.shape[0]
    for start in range(0, inner, block):
        size = min(block, inner - start)
        product = lax.dot_general(
            window[:, start : start + block],
            weight,
            (((0,), (0,)), ((), ())),
            preferred_element_type=jnp.float32,
        )
        feat[start : start + size, :] = product[:size].astype(jnp.bfloat16)


def prep(values, in_weight, gain, rows, cols, waits=()):
    channels = in_weight.shape[3]
    dims, frames, height, width = values.shape
    clip, patch = flat_inputs(values, rows, cols)
    span = patch.shape[1]
    pad = lanes_up(span + 2) - span
    patch = jnp.pad(patch, ((0, 0), (0, pad)))
    clip, patch = after((clip, patch), *waits)
    weight = jnp.pad(in_weight.reshape(9, dims, channels), ((0, 1), (0, 8 - dims), (0, 128)))
    marks = np.zeros((10, 8, channels + 128), np.float32)
    marks[0, 6, channels:] = 1.0
    weight = (weight + jnp.asarray(marks, jnp.bfloat16)).reshape(80, channels + 128)
    norm = pl.pallas_call(
        lambda *refs: prep_kernel(width + 2, *refs),
        out_shape=jax.ShapeDtypeStruct((16, channels), jnp.float32),
        scratch_shapes=[pltpu.VMEM((80, clip.shape[1]), jnp.bfloat16)],
        compiler_params=pltpu.CompilerParams(vmem_limit_bytes=(16 << 20) + 512 * clip.shape[1]),
        name="prep",
    )(clip, weight, gain.reshape(1, channels))
    return patch, weight, norm


def conv1_kernel(copy_plan, rows, cols, *refs):
    patch_ref, w_ref, norm_ref, *sources, hid_ref, stat_ref, weight, wide, act, feat, total, sems = refs
    row_len = 2 * COL
    copies = copy_plan(sources, weight, sems, 0, 9)
    for copy in copies:
        copy.start()
    features(patch_ref[...], w_ref, norm_ref, wide, act, feat)
    channels = feat.shape[1]
    count = hid_ref.shape[0]
    group = count
    for copy in copies:
        copy.wait()
    for row_tap in range(3):
        taps = weight[3 * row_tap : 3 * row_tap + 3].reshape(3 * channels, channels)
        for start in range(0, count, group):
            size = min(group, count - start)
            first = start + row_tap * row_len
            product = jnp.dot(
                act[first : first + size, :], taps, preferred_element_type=jnp.float32
            )
            if row_tap == 0:
                total[start : start + size, :] = product + feat[start : start + size, :]
            elif row_tap == 1:
                total[start : start + size, :] += product
            else:
                hid_ref[start : start + size, :] = (total[start : start + size, :] + product).astype(
                    jnp.bfloat16
                )

    place = lax.broadcasted_iota(jnp.int32, (row_len, 128), 0)
    place = jnp.where(place >= COL, place - COL, place)
    keep = ((place >= 1) & (place <= cols)).astype(jnp.float32)
    keep = jnp.concatenate([keep] * (channels // 128), axis=1)
    lines = range(row_len, (rows + 1) * row_len, row_len)
    cells = 2.0 * rows * cols
    mean = jnp.zeros((row_len, channels), jnp.float32)
    for line in lines:
        mean = mean + hid_ref[line : line + row_len, :].astype(jnp.float32)
    mean = jnp.sum(mean * keep, axis=0, keepdims=True) / cells
    square = jnp.zeros((row_len, channels), jnp.float32)
    for line in lines:
        apart = hid_ref[line : line + row_len, :].astype(jnp.float32) - mean
        square = square + apart * apart
    stat_ref[0:1, :] = mean
    stat_ref[1:2, :] = jnp.sum(square * keep, axis=0, keepdims=True)
    stat_ref[2:8, :] = jnp.zeros((6, channels), jnp.float32)


def conv2_kernel(copy_plan, stat_count, rows, cols, edge_ref, hid_ref, gain_ref, *refs):
    stat_refs, refs = refs[:stat_count], refs[stat_count:]
    *sources, out_ref, weight, wide, shifted, woven, result, sems, out_sem = refs
    row_len = 2 * COL
    channels = hid_ref.shape[1]
    copies = copy_plan(sources, weight, sems, 0, 16)
    for copy in copies:
        copy.start()

    parts = sum(ref.shape[0] for ref in stat_refs)
    cells = 2.0 * rows * cols
    means = jnp.concatenate([ref[:, 0, :] for ref in stat_refs], axis=0)
    squares = jnp.concatenate([ref[:, 1, :] for ref in stat_refs], axis=0)
    average_c = jnp.sum(means, axis=0, keepdims=True) / parts
    apart = means - average_c
    square_c = jnp.sum(squares + cells * apart * apart, axis=0, keepdims=True)
    average_c = jnp.broadcast_to(average_c, (8, channels))
    spread_c = jnp.broadcast_to(square_c, (8, channels)) / (cells * parts)
    average = group_mean(average_c)
    apart = average_c - average
    spread = group_mean(spread_c + apart * apart)
    scale = (lax.rsqrt(spread + epsilon) * gain_ref[...])[0:1, :]
    average = average[0:1, :]

    place = lax.broadcasted_iota(jnp.int32, (row_len, channels), 0)
    place = jnp.where(place >= COL, place - COL, place)
    top, bottom, left, right = (edge_ref[i].astype(jnp.float32) for i in range(4))
    keep = jnp.where(place == 0, left, jnp.where(place == cols + 1, right, 1.0))

    def normalise(line, _):
        first = pl.multiple_of(line * row_len, row_len)
        t = (hid_ref[pl.ds(first, row_len), :].astype(jnp.float32) - average) * scale
        row_keep = jnp.where(line == 0, top, jnp.where(line == rows + 1, bottom, 1.0))
        wide[...] = silu(t) * (keep * row_keep)
        for shift in range(3):
            for frame in range(2):
                to = pl.multiple_of(line * (2 * cols) + frame * cols, cols)
                shifted[pl.ds(to, cols), shift * channels : (shift + 1) * channels] = wide[
                    frame * COL + shift : frame * COL + shift + cols, :
                ].astype(jnp.bfloat16)
        return 0

    lax.fori_loop(0, rows + 2, normalise, 0)
    for copy in copies:
        copy.wait()

    step = 8
    size = step * 2 * cols

    for part in range(rows // step):
        line = part * step
        for row_phase in range(2):
            for col_phase in range(2):
                acc = None
                for row_kernel, row_offset in up_taps[row_phase]:
                    first = (line + row_offset) * (2 * cols)
                    tap = 4 * row_kernel + 2 * col_phase
                    product = jnp.dot(
                        shifted[
                            pl.ds(first, size), col_phase * channels : (col_phase + 2) * channels
                        ],
                        weight[tap : tap + 2].reshape(2 * channels, channels),
                        preferred_element_type=jnp.float32,
                    )
                    acc = product if acc is None else acc + product
                for lane in range(channels // 128):
                    woven[row_phase, lane, pl.ds(col_phase, size, stride=2), :] = acc[
                        :, 128 * lane : 128 * lane + 128
                    ]
            for y in range(step):
                for frame in range(2):
                    at = (2 * y + frame) * 2 * cols
                    for lane in range(channels // 128):
                        result[
                            frame,
                            2 * (line + y) + row_phase,
                            :,
                            128 * lane : 128 * lane + 128,
                        ] = woven[row_phase, lane, at : at + 2 * cols, :].astype(jnp.bfloat16)
        for frame in range(2):
            lines = pl.ds(2 * line, 2 * step)
            pltpu.make_async_copy(
                result.at[frame, lines], out_ref.at[frame, lines], out_sem.at[part, frame]
            ).start()
    for part in range(rows // step):
        for frame in range(2):
            lines = pl.ds(2 * step * part, 2 * step)
            pltpu.make_async_copy(
                result.at[frame, lines], out_ref.at[frame, lines], out_sem.at[part, frame]
            ).wait()


def xor_pairs(axis, bits):
    return [(i, i ^ bits) for i in range(lax.axis_size(axis))]


def tap_major(weight):
    return jnp.transpose(weight, (1, 2, 0, 3)).reshape(-1, weight.shape[0], weight.shape[3])


def paired_taps(weight):
    rows, _, _, width = weight.shape
    halves = weight.reshape(rows, 4, 2, 2, width)[:, :, ::-1, ::-1, :]
    return jnp.transpose(halves, (1, 3, 2, 0, 4)).reshape(16, rows, width)


def column_part(weight):
    width = weight.shape[2] // lax.axis_size("clip")
    return lax.dynamic_slice_in_dim(weight, lax.axis_index("clip") * width, width, axis=2)


def swap(piece):
    return lax.ppermute(piece, "px", xor_pairs("px", 1))


def whole_gather(weight):
    def plan(sources, weight, sems, first, taps):
        taps = pl.ds(first, taps)
        return [pltpu.make_async_copy(sources[0].at[taps], weight.at[taps], sems.at[first, 0])]

    return [lax.all_gather(weight, ("py", "px"), axis=1, tiled=True)], plan


def after(held, *waits):
    return lax.optimization_barrier((held, waits))[0]


def to_z(part, bits):
    return lax.ppermute(part, "py", xor_pairs("py", bits))


def to_clips(piece):
    return [piece] + [lax.ppermute(piece, "clip", xor_pairs("clip", d)) for d in (1, 2, 3)]


def both_cores(pieces):
    return [one for piece in pieces for one in (piece, swap(piece))]


def placed_plan(placed):
    sources = []
    for entry in placed:
        if not any(entry[0] is source for source in sources):
            sources.append(entry[0])
    slots = [next(i for i, source in enumerate(sources) if source is entry[0]) for entry in placed]

    def plan(refs, weight, sems, first, taps):
        core, z, clip = lax.axis_index("px"), lax.axis_index("py"), lax.axis_index("clip")
        taps = pl.ds(first, taps)
        copies = []
        for i, (slot, (_, lead, z_bits, clip_bits, core_bit)) in enumerate(zip(slots, placed)):
            ref = refs[slot]
            rows, width = ref.shape[-2:]
            row = pl.ds(pl.multiple_of((2 * (z ^ z_bits) + (core ^ core_bit)) * rows, rows), rows)
            if clip_bits is None:
                to = weight.at[taps, row, :]
            elif clip_bits >= 0:
                to = weight.at[
                    taps, row, pl.ds(pl.multiple_of((clip ^ clip_bits) * width, width), width)
                ]
            else:
                to = weight.at[taps, row, pl.ds(-(clip_bits + 1) * width, width)]
            copies.append(
                pltpu.make_async_copy(ref.at[(*lead, taps)], to, sems.at[first, i])
            )
        return copies

    return sources, plan


def code_gather(values):
    if lax.axis_size("py") != 4 or lax.axis_size("px") != 2:
        return axis_gather(axis_gather(values, "px", 3), "py", 2), values
    z, core = lax.axis_index("py"), lax.axis_index("px")
    dense = values.reshape(values.shape[0] * values.shape[1], -1)
    moved = [to_z(dense, j) for j in (1, 2, 3)]
    own, *others = [values] + [piece.reshape(values.shape) for piece in moved]
    low, high = (z & 1) != 0, (z & 2) != 0
    pairs = [
        jnp.concatenate([jnp.where(low, b, a), jnp.where(low, a, b)], axis=2)
        for a, b in ((own, others[0]), (others[1], others[2]))
    ]
    column = jnp.concatenate(
        [jnp.where(high, pairs[1], pairs[0]), jnp.where(high, pairs[0], pairs[1])], axis=2
    )
    other = swap(column.reshape(dense.shape[0], -1)).reshape(column.shape)
    whole = jnp.concatenate(
        [jnp.where(core != 0, other, column), jnp.where(core != 0, column, other)], axis=3
    )
    return whole, moved


def stat_gather(pair):
    return [pair] + [lax.ppermute(pair, "py", xor_pairs("py", j)) for j in (1, 2, 3)]


ANY = pl.BlockSpec(memory_space=pl.ANY)
WHOLE = pl.BlockSpec(memory_space=pltpu.VMEM)


def local(fsq_codes, in_weight, res_weight, up_weight, first_gain, second_gain):
    dims, frames, rows, cols = fsq_codes.shape
    channels = in_weight.shape[3]
    row_len = frames * COL
    res_taps, up_taps_own = tap_major(res_weight), paired_taps(up_weight)
    paired = tuple(lax.axis_size(axis) for axis in ("clip", "py", "px")) == (4, 4, 2)
    if paired:
        codes = code_gather(code_values(fsq_codes))
        res_part, up_part = column_part(res_taps), column_part(up_taps_own)
        res = [to_z(res_part, j) for j in (1, 2, 3)]
        res_other, up_other = (swap(after(own, codes[1])) for own in (res_taps, up_taps_own))
        waits = (res_other, up_other)
        patch, in_taps, norm = prep(codes[0], in_weight, first_gain, rows, cols, waits)
        res_spread = to_clips(after(jnp.stack(res), norm))
        up = [to_z(after(up_part, norm, *res), 2)]
        up.append(to_z(up[0], 1))
        up_near = to_z(after(up_taps_own, *res_spread), 1)
        up_spread = to_clips(after(jnp.stack(up), *res_spread))
        placed = [(res_taps, (), 0, None, 0), (res_other, (), 0, None, 1)]
        for d in range(4):
            for core, held in enumerate((res_spread[d], swap(res_spread[d]))):
                placed += [(held, (j - 1,), j, d, core) for j in (1, 2, 3)]
        res_sources, res_plan = placed_plan(placed)
    else:
        patch, in_taps, norm = prep(code_gather(code_values(fsq_codes))[0], in_weight, first_gain, rows, cols)
        res_sources, res_plan = whole_gather(res_taps)
    cells = (rows + 2) * row_len
    hidden, stat = pl.pallas_call(
        lambda *refs: conv1_kernel(res_plan, rows, cols, *refs),
        out_shape=(
            jax.ShapeDtypeStruct((cells, channels), jnp.bfloat16),
            jax.ShapeDtypeStruct((8, channels), jnp.float32),
        ),
        in_specs=[WHOLE, WHOLE, WHOLE] + [ANY] * len(res_sources),
        scratch_shapes=[
            pltpu.VMEM((9, channels, channels), jnp.bfloat16),
            pltpu.VMEM((patch.shape[1], channels), jnp.float32),
            pltpu.VMEM((cells + 2 * row_len, 3 * channels), jnp.bfloat16),
            pltpu.VMEM((cells, channels), jnp.bfloat16),
            pltpu.VMEM((cells, channels), jnp.float32),
            pltpu.SemaphoreType.DMA((1, 32)),
        ],
        compiler_params=pltpu.CompilerParams(vmem_limit_bytes=VMEM_LIMIT),
        cost_estimate=pl.CostEstimate(
            flops=2 * 9 * cells * channels * channels, bytes_accessed=12 << 20, transcendentals=0
        ),
        name="conv1",
    )(patch, in_taps, norm, *res_sources)
    if paired:
        other = swap(stat)
        up_near, *up_spread = after((up_near, *up_spread), other)
        stats = stat_gather(after(jnp.stack([stat, other]), up_near, *up_spread))
        placed = [(up_taps_own, (), 0, None, 0), (up_other, (), 0, None, 1)]
        placed += [(up_near, (), 1, None, 0), (swap(up_near), (), 1, None, 1)]
        for d in range(4):
            for core, held in enumerate((up_spread[d], swap(up_spread[d]))):
                placed += [(held, (j - 2,), j, d, core) for j in (2, 3)]
        up_sources, up_plan = placed_plan(placed)
    else:
        up_sources, up_plan = whole_gather(up_taps_own)
        stats = [axis_gather(axis_gather(stat[None], "px", 0), "py", 0)]
    py, px = lax.axis_index("py"), lax.axis_index("px")
    edges = jnp.stack(
        [py > 0, py < lax.axis_size("py") - 1, px > 0, px < lax.axis_size("px") - 1]
    ).astype(jnp.int32)
    step = 8
    return pl.pallas_call(
        lambda *refs: conv2_kernel(up_plan, len(stats), rows, cols, *refs),
        out_shape=jax.ShapeDtypeStruct((frames, 2 * rows, 2 * cols, channels), jnp.bfloat16),
        in_specs=[pl.BlockSpec(memory_space=pltpu.SMEM), WHOLE, WHOLE]
        + [WHOLE] * len(stats)
        + [ANY] * len(up_sources),
        out_specs=ANY,
        scratch_shapes=[
            pltpu.VMEM((16, channels, channels), jnp.bfloat16),
            pltpu.VMEM((row_len, channels), jnp.float32),
            pltpu.VMEM(((rows + 2) * frames * cols, 3 * channels), jnp.bfloat16),
            pltpu.VMEM((2, channels // 128, 2 * step * frames * cols, 128), jnp.float32),
            pltpu.VMEM((frames, 2 * rows, 2 * cols, channels), jnp.bfloat16),
            pltpu.SemaphoreType.DMA((1, 32)),
            pltpu.SemaphoreType.DMA((rows // step, frames)),
        ],
        compiler_params=pltpu.CompilerParams(vmem_limit_bytes=VMEM_LIMIT),
        cost_estimate=pl.CostEstimate(
            flops=2 * 16 * frames * rows * cols * channels * channels,
            bytes_accessed=16 << 20,
            transcendentals=0,
        ),
        name="conv2",
    )(edges, hidden, second_gain.reshape(1, channels), *stats, *up_sources)


def solution(mesh):
    placed = (
        P(None, "clip", "py", "px"),
        P(),
        P(("py", "px"), None, None, None),
        P(("py", "px"), None, None, None),
        P(),
        P(),
    )
    return jax.shard_map(
        local, mesh=mesh, in_specs=placed, out_specs=P("clip", "py", "px", None), check_vma=False
    )
```

```python
import jax
import jax.numpy as jnp
import numpy as np
from jax import lax
from jax.experimental import pallas as pl
from jax.experimental.pallas import tpu as pltpu
from jax.sharding import PartitionSpec as P

GROUPS = 32

fsq_levels = (8, 8, 8, 5, 5, 5)
epsilon = 1e-06
VMEM_LIMIT = 56 << 20
up_taps = (((1, 1), (3, 0)), ((0, 2), (2, 1)))

COL = 40


def axis_gather(cells, axis, dim):
    count = lax.axis_size(axis)
    me = lax.axis_index(axis)
    step = 1
    while step < count:
        other = lax.ppermute(cells, axis, [(i, i ^ step) for i in range(count)])
        upper = (me & step) != 0
        low = jnp.where(upper, other, cells)
        high = jnp.where(upper, cells, other)
        cells = jnp.concatenate([low, high], axis=dim)
        step *= 2
    return cells


def code_values(fsq_codes):
    levels = jnp.array(fsq_levels, jnp.int32).reshape(-1, 1, 1, 1)
    half_range = levels // 2
    values = (fsq_codes - half_range).astype(jnp.float32) / half_range.astype(jnp.float32)
    return values.astype(jnp.bfloat16)


def lanes_up(count):
    return (count + 127) // 128 * 128


def flat_inputs(values, rows, cols):
    dims, frames, height, width = values.shape
    py = lax.axis_index("py")
    px = lax.axis_index("px")
    clip = jnp.pad(values, ((0, 0), (0, 0), (1, 1), (1, 1)))
    inside = np.zeros((1, frames, height + 2, width + 2), np.float32)
    inside[:, :, :height, :width] = 1.0
    clip = jnp.concatenate([clip, jnp.asarray(inside, jnp.bfloat16), jnp.zeros_like(clip[:1])], axis=0)
    clip = clip.reshape(8, -1)
    clip = jnp.pad(clip, ((0, 0), (0, lanes_up(clip.shape[1]) - clip.shape[1])))

    wide = jnp.pad(values, ((0, 0), (0, 0), (3, 3), (3, 3)))
    patch = lax.dynamic_slice(
        wide, (0, 0, py * rows, px * cols), (dims, frames, rows + 6, cols + 6)
    )
    y = py * rows - 2 + jnp.arange(rows + 6)[:, None]
    x = px * cols - 2 + jnp.arange(cols + 6)[None, :]
    valid = (y >= 0) & (y < height) & (x >= 0) & (x < width)
    valid = jnp.broadcast_to(valid, (1, frames, rows + 6, cols + 6)).astype(jnp.bfloat16)
    patch = jnp.concatenate([patch, valid, jnp.zeros_like(valid)], axis=0)
    patch = jnp.pad(patch, ((0, 0), (0, 0), (0, 0), (0, COL - cols - 6)))
    patch = jnp.transpose(patch, (0, 2, 1, 3)).reshape(8, -1)
    return clip.astype(jnp.float32), patch.astype(jnp.float32)


def group_mean(row):
    lane = lax.broadcasted_iota(jnp.int32, row.shape, 1)
    width = row.shape[1]
    for step in (1, 2, 4, 8):
        row = row + jnp.where(
            (lane & step) != 0, pltpu.roll(row, step, 1), pltpu.roll(row, width - step, 1)
        )
    return row * (1.0 / 16.0)


def silu(t):
    return t * (0.5 * jnp.tanh(0.5 * t) + 0.5)


def tap_rows(flat, stride, keep=None):
    width = flat.shape[1]
    parts = []
    for tap in range(9):
        shift = (tap // 3) * stride + tap % 3
        part = flat if shift == 0 else pltpu.roll(flat, width - shift, 1)
        parts.append(part if keep is None else part * keep)
    parts.append(jnp.zeros_like(flat))
    return [
        jnp.concatenate(parts[2 * i : 2 * i + 2], axis=0).astype(jnp.bfloat16) for i in range(5)
    ]


def prep_kernel(clip_stride, clip_ref, w_ref, gain_ref, norm_ref, taps):
    channels = gain_ref.shape[1]
    for i, part in enumerate(tap_rows(clip_ref[...], clip_stride, clip_ref[6:7, :])):
        taps[16 * i : 16 * i + 16, :] = part
    moments = lax.dot_general(
        taps[...], taps[...], (((1,), (1,)), ((), ())), preferred_element_type=jnp.float32
    )
    total = moments[6:7, 6:7]
    mean_row = moments[6:7, :] / total
    mean_col = moments[:, 6:7] / total
    centred = moments / total - mean_col * mean_row
    weight32 = w_ref[:, :channels].astype(jnp.float32)
    spread_c = jnp.sum(
        weight32
        * jnp.dot(
            centred, weight32, precision=lax.Precision.HIGHEST, preferred_element_type=jnp.float32
        ),
        axis=0,
        keepdims=True,
    )
    mean_c = jnp.sum(weight32 * mean_col, axis=0, keepdims=True)
    mean_c = jnp.broadcast_to(mean_c, (8, channels))
    spread_c = jnp.broadcast_to(spread_c, (8, channels))
    average = group_mean(mean_c)
    apart = mean_c - average
    spread = jnp.maximum(group_mean(spread_c + apart * apart), 0.0)
    norm_ref[0:8, :] = average
    norm_ref[8:16, :] = lax.rsqrt(spread + epsilon) * gain_ref[...]


def features(patch, w_ref, norm_ref, wide, act, feat):
    channels = feat.shape[1]
    row_len = 2 * COL
    weight = w_ref[:, :channels]
    average = norm_ref[0:1, :]
    scale = norm_ref[8:9, :]
    span = patch.shape[1]
    window = jnp.concatenate(tap_rows(patch, row_len), axis=0)
    block = 256
    for start in range(0, span, block):
        size = min(block, span - start)
        product = lax.dot_general(
            window[:, start : start + size],
            w_ref[...],
            (((0,), (0,)), ((), ())),
            preferred_element_type=jnp.float32,
        )
        keep = product[:, channels : channels + 128]
        rounded = product[:, :channels].astype(jnp.bfloat16).astype(jnp.float32)
        active = silu((rounded - average) * scale)
        for lane in range(0, channels, 128):
            wide[start : start + size, lane : lane + 128] = active[:, lane : lane + 128] * keep
    count = act.shape[0]
    for shift in range(3):
        act[:, shift * channels : (shift + 1) * channels] = wide[shift : shift + count, :].astype(
            jnp.bfloat16
        )
    moved = pltpu.roll(patch, span - (row_len + 1), 1)
    window = jnp.concatenate(tap_rows(moved, row_len), axis=0)
    inner = feat.shape[0]
    for start in range(0, inner, block):
        size = min(block, inner - start)
        product = lax.dot_general(
            window[:, start : start + block],
            weight,
            (((0,), (0,)), ((), ())),
            preferred_element_type=jnp.float32,
        )
        feat[start : start + size, :] = product[:size].astype(jnp.bfloat16)


def prep(values, in_weight, gain, rows, cols, waits=()):
    channels = in_weight.shape[3]
    dims, frames, height, width = values.shape
    clip, patch = flat_inputs(values, rows, cols)
    span = patch.shape[1]
    pad = lanes_up(span + 2) - span
    patch = jnp.pad(patch, ((0, 0), (0, pad)))
    clip, patch = after((clip, patch), *waits)
    weight = jnp.pad(in_weight.reshape(9, dims, channels), ((0, 1), (0, 8 - dims), (0, 128)))
    marks = np.zeros((10, 8, channels + 128), np.float32)
    marks[0, 6, channels:] = 1.0
    weight = (weight + jnp.asarray(marks, jnp.bfloat16)).reshape(80, channels + 128)
    norm = pl.pallas_call(
        lambda *refs: prep_kernel(width + 2, *refs),
        out_shape=jax.ShapeDtypeStruct((16, channels), jnp.float32),
        scratch_shapes=[pltpu.VMEM((80, clip.shape[1]), jnp.bfloat16)],
        compiler_params=pltpu.CompilerParams(vmem_limit_bytes=(16 << 20) + 512 * clip.shape[1]),
        name="prep",
    )(clip, weight, gain.reshape(1, channels))
    return patch, weight, norm


def conv1_kernel(copy_plan, rows, cols, *refs):
    patch_ref, w_ref, norm_ref, *sources, hid_ref, stat_ref, weight, wide, act, feat, total, sems = refs
    row_len = 2 * COL
    copies = copy_plan(sources, weight, sems, 0, 9)
    for copy in copies:
        copy.start()
    features(patch_ref[...], w_ref, norm_ref, wide, act, feat)
    channels = feat.shape[1]
    count = hid_ref.shape[0]
    group = count
    for copy in copies:
        copy.wait()
    for row_tap in range(3):
        taps = weight[3 * row_tap : 3 * row_tap + 3].reshape(3 * channels, channels)
        for start in range(0, count, group):
            size = min(group, count - start)
            first = start + row_tap * row_len
            product = jnp.dot(
                act[first : first + size, :], taps, preferred_element_type=jnp.float32
            )
            if row_tap == 0:
                total[start : start + size, :] = product + feat[start : start + size, :]
            elif row_tap == 1:
                total[start : start + size, :] += product
            else:
                hid_ref[start : start + size, :] = (total[start : start + size, :] + product).astype(
                    jnp.bfloat16
                )

    place = lax.broadcasted_iota(jnp.int32, (row_len, 128), 0)
    place = jnp.where(place >= COL, place - COL, place)
    keep = ((place >= 1) & (place <= cols)).astype(jnp.float32)
    keep = jnp.concatenate([keep] * (channels // 128), axis=1)
    lines = range(row_len, (rows + 1) * row_len, row_len)
    cells = 2.0 * rows * cols
    mean = jnp.zeros((row_len, channels), jnp.float32)
    for line in lines:
        mean = mean + hid_ref[line : line + row_len, :].astype(jnp.float32)
    mean = jnp.sum(mean * keep, axis=0, keepdims=True) / cells
    square = jnp.zeros((row_len, channels), jnp.float32)
    for line in lines:
        apart = hid_ref[line : line + row_len, :].astype(jnp.float32) - mean
        square = square + apart * apart
    stat_ref[0:1, :] = mean
    stat_ref[1:2, :] = jnp.sum(square * keep, axis=0, keepdims=True)
    stat_ref[2:8, :] = jnp.zeros((6, channels), jnp.float32)


def conv2_kernel(copy_plan, stat_count, rows, cols, hid_ref, gain_ref, *refs):
    stat_refs, refs = refs[:stat_count], refs[stat_count:]
    *sources, out_ref, weight, wide, shifted, woven, result, sems, out_sem = refs
    row_len = 2 * COL
    channels = hid_ref.shape[1]
    copies = copy_plan(sources, weight, sems, 0, 16)
    for copy in copies:
        copy.start()

    parts = sum(ref.shape[0] for ref in stat_refs)
    cells = 2.0 * rows * cols
    means = jnp.concatenate([ref[:, 0, :] for ref in stat_refs], axis=0)
    squares = jnp.concatenate([ref[:, 1, :] for ref in stat_refs], axis=0)
    average_c = jnp.sum(means, axis=0, keepdims=True) / parts
    apart = means - average_c
    square_c = jnp.sum(squares + cells * apart * apart, axis=0, keepdims=True)
    average_c = jnp.broadcast_to(average_c, (8, channels))
    spread_c = jnp.broadcast_to(square_c, (8, channels)) / (cells * parts)
    average = group_mean(average_c)
    apart = average_c - average
    spread = group_mean(spread_c + apart * apart)
    scale = (lax.rsqrt(spread + epsilon) * gain_ref[...])[0:1, :]
    average = average[0:1, :]

    place = lax.broadcasted_iota(jnp.int32, (row_len, channels), 0)
    place = jnp.where(place >= COL, place - COL, place)
    py, px = lax.axis_index("py"), lax.axis_index("px")
    inside = (py > 0, py < lax.axis_size("py") - 1, px > 0, px < lax.axis_size("px") - 1)
    top, bottom, left, right = (jnp.where(one, 1.0, 0.0) for one in inside)
    keep = jnp.where(place == 0, left, jnp.where(place == cols + 1, right, 1.0))

    def normalise(line, _):
        first = pl.multiple_of(line * row_len, row_len)
        t = (hid_ref[pl.ds(first, row_len), :].astype(jnp.float32) - average) * scale
        row_keep = jnp.where(line == 0, top, jnp.where(line == rows + 1, bottom, 1.0))
        wide[...] = silu(t) * (keep * row_keep)
        for shift in range(3):
            for frame in range(2):
                to = pl.multiple_of(line * (2 * cols) + frame * cols, cols)
                shifted[pl.ds(to, cols), shift * channels : (shift + 1) * channels] = wide[
                    frame * COL + shift : frame * COL + shift + cols, :
                ].astype(jnp.bfloat16)
        return 0

    lax.fori_loop(0, rows + 2, normalise, 0)
    for copy in copies:
        copy.wait()

    step = 16
    size = step * 2 * cols

    for part in range(rows // step):
        line = part * step
        for row_phase in range(2):
            for col_phase in range(2):
                acc = None
                for row_kernel, row_offset in up_taps[row_phase]:
                    first = (line + row_offset) * (2 * cols)
                    for col_kernel, col_offset in up_taps[col_phase]:
                        product = jnp.dot(
                            shifted[
                                pl.ds(first, size),
                                col_offset * channels : (col_offset + 1) * channels,
                            ],
                            weight[4 * row_kernel + col_kernel],
                            preferred_element_type=jnp.float32,
                        )
                        acc = product if acc is None else acc + product
                for lane in range(channels // 128):
                    woven[row_phase, lane, pl.ds(col_phase, size, stride=2), :] = acc[
                        :, 128 * lane : 128 * lane + 128
                    ]
            for y in range(step):
                for frame in range(2):
                    at = (2 * y + frame) * 2 * cols
                    for lane in range(channels // 128):
                        result[
                            frame,
                            2 * (line + y) + row_phase,
                            :,
                            128 * lane : 128 * lane + 128,
                        ] = woven[row_phase, lane, at : at + 2 * cols, :].astype(jnp.bfloat16)
        for frame in range(2):
            lines = pl.ds(2 * line, 2 * step)
            pltpu.make_async_copy(
                result.at[frame, lines], out_ref.at[frame, lines], out_sem.at[part, frame]
            ).start()
    for part in range(rows // step):
        for frame in range(2):
            lines = pl.ds(2 * step * part, 2 * step)
            pltpu.make_async_copy(
                result.at[frame, lines], out_ref.at[frame, lines], out_sem.at[part, frame]
            ).wait()


def xor_pairs(axis, bits):
    return [(i, i ^ bits) for i in range(lax.axis_size(axis))]


def tap_major(weight):
    return jnp.transpose(weight, (1, 2, 0, 3)).reshape(-1, weight.shape[0], weight.shape[3])


def column_part(weight):
    width = weight.shape[2] // lax.axis_size("clip")
    return lax.dynamic_slice_in_dim(weight, lax.axis_index("clip") * width, width, axis=2)


def swap(piece):
    return lax.ppermute(piece, "px", xor_pairs("px", 1))


def whole_gather(weight):
    def plan(sources, weight, sems, first, taps):
        taps = pl.ds(first, taps)
        return [pltpu.make_async_copy(sources[0].at[taps], weight.at[taps], sems.at[first, 0])]

    return [lax.all_gather(weight, ("py", "px"), axis=1, tiled=True)], plan


def after(held, *waits):
    return lax.optimization_barrier((held, waits))[0]


def to_z(part, bits):
    return lax.ppermute(part, "py", xor_pairs("py", bits))


def to_clips(piece):
    return [piece] + [lax.ppermute(piece, "clip", xor_pairs("clip", d)) for d in (1, 2, 3)]


def both_cores(pieces):
    return [one for piece in pieces for one in (piece, swap(piece))]


def placed_plan(placed):
    sources = []
    for entry in placed:
        if not any(entry[0] is source for source in sources):
            sources.append(entry[0])
    slots = [next(i for i, source in enumerate(sources) if source is entry[0]) for entry in placed]

    def plan(refs, weight, sems, first, taps):
        core, z, clip = lax.axis_index("px"), lax.axis_index("py"), lax.axis_index("clip")
        taps = pl.ds(first, taps)
        copies = []
        for i, (slot, (_, lead, z_bits, clip_bits, core_bit)) in enumerate(zip(slots, placed)):
            ref = refs[slot]
            rows, width = ref.shape[-2:]
            row = pl.ds(pl.multiple_of((2 * (z ^ z_bits) + (core ^ core_bit)) * rows, rows), rows)
            if clip_bits is None:
                to = weight.at[taps, row, :]
            elif clip_bits >= 0:
                to = weight.at[
                    taps, row, pl.ds(pl.multiple_of((clip ^ clip_bits) * width, width), width)
                ]
            else:
                to = weight.at[taps, row, pl.ds(-(clip_bits + 1) * width, width)]
            copies.append(
                pltpu.make_async_copy(ref.at[(*lead, taps)], to, sems.at[first, i])
            )
        return copies

    return sources, plan


def code_gather(values):
    if lax.axis_size("py") != 4 or lax.axis_size("px") != 2:
        return axis_gather(axis_gather(values, "px", 3), "py", 2), values
    z, core = lax.axis_index("py"), lax.axis_index("px")
    dense = values.reshape(values.shape[0] * values.shape[1], -1)
    moved = [to_z(dense, j) for j in (1, 2, 3)]
    own, *others = [values] + [piece.reshape(values.shape) for piece in moved]
    low, high = (z & 1) != 0, (z & 2) != 0
    pairs = [
        jnp.concatenate([jnp.where(low, b, a), jnp.where(low, a, b)], axis=2)
        for a, b in ((own, others[0]), (others[1], others[2]))
    ]
    column = jnp.concatenate(
        [jnp.where(high, pairs[1], pairs[0]), jnp.where(high, pairs[0], pairs[1])], axis=2
    )
    other = swap(column.reshape(dense.shape[0], -1)).reshape(column.shape)
    whole = jnp.concatenate(
        [jnp.where(core != 0, other, column), jnp.where(core != 0, column, other)], axis=3
    )
    return whole, moved


def stat_gather(pair):
    return [pair] + [lax.ppermute(pair, "py", xor_pairs("py", j)) for j in (1, 2, 3)]


ANY = pl.BlockSpec(memory_space=pl.ANY)
WHOLE = pl.BlockSpec(memory_space=pltpu.VMEM)


def local(fsq_codes, in_weight, res_weight, up_weight, first_gain, second_gain):
    dims, frames, rows, cols = fsq_codes.shape
    channels = in_weight.shape[3]
    row_len = frames * COL
    res_taps, up_taps_own = tap_major(res_weight), tap_major(up_weight)
    paired = tuple(lax.axis_size(axis) for axis in ("clip", "py", "px")) == (4, 4, 2)
    if paired:
        codes = code_gather(code_values(fsq_codes))
        res_part, up_part = column_part(res_taps), column_part(up_taps_own)
        res = [to_z(res_part, j) for j in (1, 2, 3)]
        res_other, up_other = (swap(after(own, codes[1])) for own in (res_taps, up_taps_own))
        waits = (res_other, up_other)
        patch, in_taps, norm = prep(codes[0], in_weight, first_gain, rows, cols, waits)
        res_spread = to_clips(after(jnp.stack(res), norm))
        up = [to_z(after(up_part, norm, *res), 2)]
        up.append(to_z(up[0], 1))
        up_near = to_z(after(up_taps_own, *res_spread), 1)
        up_spread = to_clips(after(jnp.stack(up), *res_spread))
        placed = [(res_taps, (), 0, None, 0), (res_other, (), 0, None, 1)]
        for d in range(4):
            for core, held in enumerate((res_spread[d], swap(res_spread[d]))):
                placed += [(held, (j - 1,), j, d, core) for j in (1, 2, 3)]
        res_sources, res_plan = placed_plan(placed)
    else:
        patch, in_taps, norm = prep(code_gather(code_values(fsq_codes))[0], in_weight, first_gain, rows, cols)
        res_sources, res_plan = whole_gather(res_taps)
    cells = (rows + 2) * row_len
    hidden, stat = pl.pallas_call(
        lambda *refs: conv1_kernel(res_plan, rows, cols, *refs),
        out_shape=(
            jax.ShapeDtypeStruct((cells, channels), jnp.bfloat16),
            jax.ShapeDtypeStruct((8, channels), jnp.float32),
        ),
        in_specs=[WHOLE, WHOLE, WHOLE] + [ANY] * len(res_sources),
        scratch_shapes=[
            pltpu.VMEM((9, channels, channels), jnp.bfloat16),
            pltpu.VMEM((patch.shape[1], channels), jnp.float32),
            pltpu.VMEM((cells + 2 * row_len, 3 * channels), jnp.bfloat16),
            pltpu.VMEM((cells, channels), jnp.bfloat16),
            pltpu.VMEM((cells, channels), jnp.float32),
            pltpu.SemaphoreType.DMA((1, 32)),
        ],
        compiler_params=pltpu.CompilerParams(vmem_limit_bytes=VMEM_LIMIT),
        cost_estimate=pl.CostEstimate(
            flops=2 * 9 * cells * channels * channels, bytes_accessed=12 << 20, transcendentals=0
        ),
        name="conv1",
    )(patch, in_taps, norm, *res_sources)
    if paired:
        other = swap(stat)
        up_near, *up_spread = after((up_near, *up_spread), other)
        stats = stat_gather(after(jnp.stack([stat, other]), up_near, *up_spread))
        placed = [(up_taps_own, (), 0, None, 0), (up_other, (), 0, None, 1)]
        placed += [(up_near, (), 1, None, 0), (swap(up_near), (), 1, None, 1)]
        for d in range(4):
            for core, held in enumerate((up_spread[d], swap(up_spread[d]))):
                placed += [(held, (j - 2,), j, d, core) for j in (2, 3)]
        up_sources, up_plan = placed_plan(placed)
    else:
        up_sources, up_plan = whole_gather(up_taps_own)
        stats = [axis_gather(axis_gather(stat[None], "px", 0), "py", 0)]
    step = 16
    return pl.pallas_call(
        lambda *refs: conv2_kernel(up_plan, len(stats), rows, cols, *refs),
        out_shape=jax.ShapeDtypeStruct((frames, 2 * rows, 2 * cols, channels), jnp.bfloat16),
        in_specs=[WHOLE, WHOLE]
        + [WHOLE] * len(stats)
        + [ANY] * len(up_sources),
        out_specs=ANY,
        scratch_shapes=[
            pltpu.VMEM((16, channels, channels), jnp.bfloat16),
            pltpu.VMEM((row_len, channels), jnp.float32),
            pltpu.VMEM(((rows + 2) * frames * cols, 3 * channels), jnp.bfloat16),
            pltpu.VMEM((2, channels // 128, 2 * step * frames * cols, 128), jnp.float32),
            pltpu.VMEM((frames, 2 * rows, 2 * cols, channels), jnp.bfloat16),
            pltpu.SemaphoreType.DMA((1, 32)),
            pltpu.SemaphoreType.DMA((rows // step, frames)),
        ],
        compiler_params=pltpu.CompilerParams(vmem_limit_bytes=VMEM_LIMIT),
        cost_estimate=pl.CostEstimate(
            flops=2 * 16 * frames * rows * cols * channels * channels,
            bytes_accessed=16 << 20,
            transcendentals=0,
        ),
        name="conv2",
    )(hidden, second_gain.reshape(1, channels), *stats, *up_sources)


def solution(mesh):
    placed = (
        P(None, "clip", "py", "px"),
        P(),
        P(("py", "px"), None, None, None),
        P(("py", "px"), None, None, None),
        P(),
        P(),
    )
    return jax.shard_map(
        local, mesh=mesh, in_specs=placed, out_specs=P("clip", "py", "px", None), check_vma=False
    )
```
